128 devices in a mesh: dom: 32 (over z, y, core), sub: 4 (over x).
Axes of the slice: x: 4, y: 4, z: 4, core: 2. Of those that a mesh axis runs over, the one named last changes fastest.
Arguments:
- displacement: float32 [3, 512, 289], P(None, ('dom', 'sub')), may hold values from -6 to 6
- macro_modulus: float32 [8, 131072], P(None, ('dom', 'sub')), may hold values from 0.5 to 4
- damaged_count: int32 [128], P(('dom', 'sub')), may hold values from 1 to 64, 4096 in all
- damaged_points: int32 [128, 64], P(('dom', 'sub')), may hold values from 0 to 8191, as said below
- damage: bfloat16 [8192, 4096], P(('dom', 'sub')), may hold values from 0 to 0.59765625
- voxel_modulus: bfloat16 [8192, 4096], P(('dom', 'sub')), may hold values from 0.5 to 4
Outputs:
- nodal_force: float32 [3, 512, 289], P(None, ('dom', 'sub'))
- new_damage: bfloat16 [8192, 4096], P(('dom', 'sub'))
The draws below stay inside these ranges and needn't reach their ends.
Inputs may be any that keep to these rules, and one draw needn't show every extreme that they name: `damaged_count`: the counts of all partitions sum to 4096, and the largest is 64. `damaged_points`: each row names 64 different points of its partition; the first damaged_count of them are the damaged ones; partition 0 lists point 0 and point 8 * 4 * 16^2 - 1.
All inputs are finite; a program needn't handle non-finite values. No bound on the sum of `damaged_count` on one device may be relied on, other than what follows from the above.
Results may differ from the reference program's by a relative error of at most 0.0055.
Values may be sent and summed in bfloat16 or wider, within the bound.
No kernel may reach another device: no remote copies, remote signals or barrier semaphores. Data moves between devices by JAX's collectives and lax.ppermute only.
A program may use at most 64 MiB of HBM per device.

```python
import math
import jax
import jax.numpy as jnp
import numpy as np
from jax import lax

CELL = 16
SWEEPS = 2
EXY = 16
LZ = 4
DMG_DEV = 64
DOMAINS = 128
NZ = 512
NODES = 289
ELEMS = 131072
SLOTS = 8192
DMG_SUM = 4096
VOX = 4096


def draw_damaged_points(key, part):
    point_total = 8 * LZ * EXY * EXY
    ceiling = 2 ** 30 // point_total
    scores = jax.random.randint(key, (DOMAINS, point_total), 0, ceiling) * point_total + jnp.arange(point_total)[None, :]
    scores = scores.at[0, 0].set(ceiling * point_total).at[0, point_total - 1].set(ceiling * point_total + 1)
    top_values, picked = lax.top_k(scores, DMG_DEV)
    return picked.astype(jnp.int32)


def block_levels(rng, extent, pieces, low, top_value):
    level, own = 1.0, jax.random.fold_in(rng, 6)
    for position, parts in pieces:
        steps = jnp.exp(jax.random.uniform(jax.random.fold_in(own, position), (parts,), jnp.float32, low / len(pieces), top_value / len(pieces)))
        level = level * jnp.repeat(steps, extent[position] // parts).reshape([-1 if axis == position else 1 for axis in range(len(extent))])
    return level


def split_up(number_of, total, reach, slope):
    portions = [(1 << 20) // math.isqrt(standing ** slope) + 1 for standing in range(2, number_of + 1)]
    rest, holding = total - reach - (number_of - 1), [1] * (number_of - 1)
    while rest > 0:
        free = [i for i in range(number_of - 1) if holding[i] < reach]
        pool, remaining = sum([portions[i] for i in free]), rest
        for i in free:
            addition = min(reach - holding[i], max(1, remaining * portions[i] // pool), rest)
            holding[i] = holding[i] + addition
            rest = rest - addition
    return np.array([reach] + holding)


def ragged_sizes(stream_key, amount, total, most, slope):
    if amount == 2:
        one = jax.random.randint(stream_key, (), max(1, total - most), min(most, total - 1) + 1)
        return jnp.stack([one, total - one])
    lengths = jnp.asarray(split_up(amount, total, most, slope), jnp.int32)
    couples = (amount - 1) // 2
    donor, receiver = lengths[1:1 + 2 * couples:2], lengths[2:2 + 2 * couples:2]
    room = jnp.minimum(donor - 1, most - receiver)
    shifted = jax.random.randint(jax.random.fold_in(stream_key, 1), (couples,), 0, 1 << 20) % (room + 1)
    lengths = lengths.at[1:1 + 2 * couples:2].set(donor - shifted).at[2:2 + 2 * couples:2].set(receiver + shifted)
    return lengths[jax.random.permutation(jax.random.fold_in(stream_key, 2), amount)]


def noise(stream_key, extent, scale, reach, cuts=(), kind=jnp.bfloat16):
    values = jax.random.normal(stream_key, extent, jnp.float32) * scale
    if len(cuts) > 0:
        values = block_levels(stream_key, extent, cuts, -0.22, 0.18) * values
    return jnp.clip(values, min=-reach, max=reach).astype(kind)


def setup_inputs(seed: int = 0) -> dict:
    seeds = jax.random.split(jax.random.key(seed), 7)
    return {
        "displacement": noise(seeds[0], (3, NZ, NODES), 1.0, 6.0, ((1, 128),), jnp.float32),
        "macro_modulus": jnp.clip(jnp.exp(math.log(4.0) - 2.0794415 * jax.random.uniform(seeds[1], (8, ELEMS), jnp.float32) ** block_levels(seeds[1], (8, ELEMS), ((1, 128),), -0.2, 0.2)), 0.5, 4.0),
        "damaged_count": ragged_sizes(seeds[2], DOMAINS, DMG_SUM, DMG_DEV, 2).astype(jnp.int32),
        "damaged_points": draw_damaged_points(jax.random.fold_in(seeds[6], 71), 0),
        "damage": jnp.clip(0.59765625 * jax.random.uniform(seeds[4], (SLOTS, VOX), jnp.float32) ** block_levels(seeds[4], (SLOTS, VOX), ((0, 128),), -0.2, 0.2), 0.0, 0.59765625).astype(jnp.bfloat16),
        "voxel_modulus": jnp.clip(jnp.exp(math.log(4.0) - 2.0794415 * jax.random.uniform(seeds[5], (SLOTS, VOX), jnp.float32) ** block_levels(seeds[5], (SLOTS, VOX), ((0, 128),), -0.2, 0.2)), 0.5, 4.0).astype(jnp.bfloat16),
    }


lam_hat = 0.2 / 0.72
mu_hat = 1.0 / 2.4
ref_modulus = 2.0
kappa_sq = 4.0
voigt_pairs = ((0, 0), (1, 1), (2, 2), (1, 2), (0, 2), (0, 1))

def shape_table():
    gauss_coord = 1.0 / math.sqrt(3.0)
    gradients = np.zeros((8, 8, 3), np.float32)
    for corner in range(8):
        corner_signs = [2 * (corner >> axis_no & 1) - 1 for axis_no in range(3)]
        for gauss_no in range(8):
            gauss_coords = [(2 * (gauss_no >> axis_no & 1) - 1) * gauss_coord for axis_no in range(3)]
            factor = [(1.0 + corner_signs[axis_no] * gauss_coords[axis_no]) / 2.0 for axis_no in range(3)]
            for direction in range(3):
                entry_value = float(corner_signs[direction])
                for other_dir in range(3):
                    if other_dir != direction:
                        entry_value = entry_value * factor[other_dir]
                gradients[corner, gauss_no, direction] = entry_value
    return gradients

def element_strain(node_grid, layers, side):
    gradients = jnp.asarray(shape_table())
    corner_list = []
    for corner in range(8):
        off_x, off_y, off_z = (corner & 1, corner >> 1 & 1, corner >> 2 & 1)
        piece = node_grid[:, off_z:off_z + layers, off_y:off_y + side, off_x:off_x + side]
        corner_list.append(piece.reshape(3, layers * side * side))
    stacked = jnp.stack(corner_list)
    displ_grad = jnp.einsum('cie,cqj->ijqe', stacked, gradients, precision=lax.Precision.HIGHEST)
    return jnp.stack([0.5 * (displ_grad[first_dim, second_dim] + displ_grad[second_dim, first_dim]) for first_dim, second_dim in voigt_pairs])

def nodal_forces(stress, layers, side):
    gradients = jnp.asarray(shape_table())
    tensor = jnp.stack([jnp.stack([stress[0], stress[5], stress[4]]), jnp.stack([stress[5], stress[1], stress[3]]), jnp.stack([stress[4], stress[3], stress[2]])])
    contrib = 0.125 * jnp.einsum('ijqe,cqj->cie', tensor, gradients, precision=lax.Precision.HIGHEST)
    node_grid = jnp.zeros((3, layers + 1, side + 1, side + 1), jnp.float32)
    for corner in range(8):
        off_x, off_y, off_z = (corner & 1, corner >> 1 & 1, corner >> 2 & 1)
        node_grid = node_grid.at[:, off_z:off_z + layers, off_y:off_y + side, off_x:off_x + side].add(contrib[corner].reshape(3, layers, side, side))
    return node_grid

def elastic_list(components, modulus):
    trace_sum = components[0] + components[1] + components[2]
    result = []
    for comp in range(6):
        inner = 2.0 * mu_hat * components[comp]
        if comp < 3:
            inner = inner + lam_hat * trace_sum
        result.append(modulus * inner)
    return result

def voxel_update(components, old_damage, modulus):
    energy = components[0] ** 2 + components[1] ** 2 + components[2] ** 2 + 2.0 * (components[3] ** 2 + components[4] ** 2 + components[5] ** 2)
    damage_now = jnp.maximum(old_damage, energy / (energy + kappa_sq))
    stress = elastic_list(components, (1.0 - damage_now) * modulus)
    medium = elastic_list(components, ref_modulus)
    polarization = [stress[comp] - medium[comp] for comp in range(6)]
    return (stress, polarization, damage_now)

def green_apply(components, freq_x, freq_y, freq_z):
    wave_vec = (freq_x, freq_y, freq_z)
    square = freq_x * freq_x + freq_y * freq_y + freq_z * freq_z
    inverse = jnp.where(square > 0.5, 1.0 / jnp.maximum(square, 1.0), 0.0)
    tensor = ((components[0], components[5], components[4]), (components[5], components[1], components[3]), (components[4], components[3], components[2]))
    traction = [tensor[row_no][0] * freq_x + tensor[row_no][1] * freq_y + tensor[row_no][2] * freq_z for row_no in range(3)]
    along_wave = freq_x * traction[0] + freq_y * traction[1] + freq_z * traction[2]
    lam_ref = ref_modulus * lam_hat
    mu_ref = ref_modulus * mu_hat
    coupling = (lam_ref + mu_ref) / (mu_ref * (lam_ref + 2.0 * mu_ref))
    amplitude = [inverse * traction[row_no] / mu_ref - coupling * along_wave * inverse * inverse * wave_vec[row_no] for row_no in range(3)]
    return [0.5 * (wave_vec[first_dim] * amplitude[second_dim] + wave_vec[second_dim] * amplitude[first_dim]) for first_dim, second_dim in voigt_pairs]

def narrow(values):
    return lax.optimization_barrier(values.astype(jnp.bfloat16)).astype(jnp.float32)

def cell_block(macro, old_damage, modulus):
    cell_side = CELL
    cell_total = old_damage.shape[0]
    steps_index = jnp.arange(cell_side).astype(jnp.int32)
    signed = jnp.where(steps_index < cell_side // 2, steps_index, steps_index - cell_side).astype(jnp.float32)
    freq_x = signed[None, :, None, None]
    freq_y = signed[None, None, :, None]
    freq_z = jnp.arange(cell_side // 2 + 1).astype(jnp.float32)[None, None, None, :]
    strain_now = jnp.broadcast_to(macro[:, :, None], (cell_total, 6, VOX))
    for sweep_no in range(SWEEPS):
        components = [strain_now[:, comp] for comp in range(6)]
        stress, polarization, damage_now = voxel_update(components, old_damage, modulus)
        spectra = [jnp.fft.rfftn(narrow(part_field).reshape(cell_total, cell_side, cell_side, cell_side), axes=(1, 2, 3)) for part_field in polarization]
        real_green = green_apply([spectrum.real for spectrum in spectra], freq_x, freq_y, freq_z)
        imag_green = green_apply([spectrum.imag for spectrum in spectra], freq_x, freq_y, freq_z)
        back = [jnp.fft.irfftn(narrow(real_green[comp]) + 1j * narrow(imag_green[comp]), s=(cell_side, cell_side, cell_side), axes=(1, 2, 3)).reshape(cell_total, VOX) for comp in range(6)]
        strain_now = jnp.stack([macro[:, comp:comp + 1] - back[comp] for comp in range(6)], axis=1)
    components = [strain_now[:, comp] for comp in range(6)]
    stress, polarization, damage_now = voxel_update(components, old_damage, modulus)
    mean_stress = jnp.stack([lax.optimization_barrier(jnp.mean(stress[comp], axis=1)) for comp in range(6)], axis=1)
    return (damage_now, mean_stress)

def reference(displacement, macro_modulus, damaged_count, damaged_points, damage, voxel_modulus):
    part_total = damaged_count.shape[0]
    layers = displacement.shape[1]
    base_layer = jnp.zeros((3, 1, displacement.shape[2]), displacement.dtype)
    node_grid = jnp.concatenate([base_layer, displacement], axis=1).reshape(3, layers + 1, EXY + 1, EXY + 1)
    macro_strain = element_strain(node_grid, layers, EXY)
    elem_total = macro_strain.shape[2]
    elastic_stress = jnp.stack(elastic_list([macro_strain[comp] for comp in range(6)], macro_modulus)).reshape(6, 8 * elem_total)
    flat_strain = macro_strain.reshape(6, 8 * elem_total)
    per_part = LZ * EXY * EXY
    slot_index = jnp.arange(DMG_DEV).astype(jnp.int32)
    is_live = (slot_index[None, :] < damaged_count[:, None]).reshape(-1)
    gauss_no = damaged_points // per_part
    element = jnp.arange(part_total).astype(jnp.int32)[:, None] * per_part + damaged_points % per_part
    column = (gauss_no * elem_total + element).astype(jnp.int32).reshape(-1)
    cell_strain = flat_strain[:, column].T.astype(jnp.bfloat16)

    def per_partition(inputs):
        macro, old_damage, modulus = inputs
        return cell_block(macro.astype(jnp.float32), old_damage.astype(jnp.float32), modulus.astype(jnp.float32))
    new_dmg, cell_stress = lax.map(per_partition, (cell_strain.reshape(part_total, DMG_DEV, 6), damage.reshape(part_total, DMG_DEV, VOX), voxel_modulus.reshape(part_total, DMG_DEV, VOX)))
    new_damage = jnp.where(is_live[:, None], new_dmg.reshape(SLOTS, VOX).astype(jnp.bfloat16), damage)
    cell_rounded = cell_stress.reshape(SLOTS, 6).astype(jnp.bfloat16).astype(jnp.float32)
    target = jnp.where(is_live, column, 8 * elem_total).astype(jnp.int32)
    point_stress = elastic_stress.at[:, target].set(cell_rounded.T, mode='drop')
    force_grid = nodal_forces(point_stress.reshape(6, 8, elem_total), layers, EXY)
    nodal_force = force_grid[:, 1:].reshape(3, layers, (EXY + 1) * (EXY + 1))
    return (nodal_force, new_damage)
```

```python
import math

import jax
import jax.numpy as jnp
import ml_dtypes
import numpy as np
from jax import lax
from jax.experimental import pallas as pl
from jax.experimental.pallas import tpu as pltpu
from jax.sharding import PartitionSpec as P

CELL = 16
EXY = 16
VOX = 4096
SLOTS = 64
GROUP = 16
LAYERS = 4
NODES = 289
WIDE = 384
ROW = EXY + 1

lam_hat = 0.2 / 0.72
mu_hat = 1.0 / 2.4
ref_modulus = 2.0
kappa_sq = 4.0
voigt_pairs = ((0, 0), (1, 1), (2, 2), (1, 2), (0, 2), (0, 1))
odd_in_x = (False, False, False, False, True, True)
table_scale = 1.132805
entry_pairs = [(k, m) for k in range(6) for m in range(k, 6)]
f32 = jnp.float32
bf16 = jnp.bfloat16
shifts = (0, 1, ROW, ROW + 1)


def shape_table():
    gauss_coord = 1.0 / math.sqrt(3.0)
    gradients = np.zeros((8, 8, 3), np.float32)
    for corner in range(8):
        signs = [2 * (corner >> d & 1) - 1 for d in range(3)]
        for gauss_no in range(8):
            coords = [(2 * (gauss_no >> d & 1) - 1) * gauss_coord for d in range(3)]
            factor = [(1.0 + signs[d] * coords[d]) / 2.0 for d in range(3)]
            for direction in range(3):
                value = float(signs[direction])
                for other in range(3):
                    if other != direction:
                        value = value * factor[other]
                gradients[corner, gauss_no, direction] = value
    return gradients


def macro_tables():
    gradients = shape_table().astype(np.float64)
    strain = np.zeros((LAYERS, 6, 8, 3, 4, 8))
    force = np.zeros((3, 4, 8, LAYERS, 6, 8))
    for layer in range(LAYERS):
        for corner in range(8):
            node_layer = layer + (corner >> 2)
            row = 4 if node_layer == 0 else node_layer - 1
            shift = corner & 3
            for k, (a, b) in enumerate(voigt_pairs):
                strain[layer, k, :, a, shift, row] += 0.5 * gradients[corner, :, b]
                strain[layer, k, :, b, shift, row] += 0.5 * gradients[corner, :, a]
                force[a, shift, row, layer, k, :] += 0.125 * gradients[corner, :, b]
                if a != b:
                    force[b, shift, row, layer, k, :] += 0.125 * gradients[corner, :, a]
    return (
        strain.reshape(LAYERS * 48, 96).astype(np.float32),
        force.reshape(96, LAYERS * 48).astype(np.float32),
    )


def spread_table():
    table = np.zeros((EXY * EXY, WIDE), np.float32)
    for y in range(EXY):
        for x in range(EXY):
            table[y * EXY + x, y * ROW + x] = 1.0
    return table


def green_matrix(n):
    n = np.asarray(n, np.float64)
    m = n @ n
    out = np.zeros((6, 6))
    if m == 0:
        return out
    lam_ref, mu_ref = ref_modulus * lam_hat, ref_modulus * mu_hat
    coupling = (lam_ref + mu_ref) / (mu_ref * (lam_ref + 2.0 * mu_ref))
    for col, (a, b) in enumerate(voigt_pairs):
        t = np.zeros((3, 3))
        t[a, b] = t[b, a] = 1.0
        u = t @ n
        amp = u / (mu_ref * m) - coupling * (n @ u) * n / m**2
        for k, (c, d) in enumerate(voigt_pairs):
            out[k, col] = 0.5 * (n[c] * amp[d] + n[d] * amp[c])
    return out


def lane_modes():
    modes = []
    for kz in range(1, 8):
        for ky in range(16):
            modes += [(ky, kz, 0), (ky, kz, 1)]
    for kz in (0, 8):
        for ky in range(1, 8):
            modes += [(ky, kz, 0), (ky, kz, 1)]
        modes += [(0, kz, 2), (8, kz, 2)]
    return modes


def spectral_tables():
    side = np.arange(16)
    modes = lane_modes()
    y, z = side.repeat(16), np.tile(side, 16)
    first = np.zeros((256, 256))
    second = np.zeros((256, 256))
    weight = np.zeros(256)
    for lane, (ky, kz, kind) in enumerate(modes):
        phase = 2 * np.pi * ((y * ky + z * kz) % 16) / 16
        first[:, lane] = np.sin(phase) if kind == 1 else np.cos(phase)
        second[:, lane] = (-np.sin(phase), np.cos(phase), np.cos(phase))[kind]
        weight[lane] = 1.0 if kind == 2 else 2.0
    rows = np.zeros((16, 16))
    row_weight = np.full(16, 2.0)
    row_weight[[0, 8]] = 1.0
    for row in range(16):
        k = row if row < 9 else row - 8
        phase = 2 * np.pi * (side * k % 16) / 16
        rows[row] = np.cos(phase) if row < 9 else np.sin(phase)

    def rounded(table):
        table = np.where(np.abs(table) < 1e-9, 0.0, table)
        return (table * table_scale).astype(ml_dtypes.bfloat16)

    eye = np.eye(GROUP)
    forward_x = rounded(np.kron(rows, eye))
    inverse_x = rounded(np.kron((rows * row_weight[:, None]).T, eye))
    signed = np.where(side < 8, side, side - 16)

    def green_at(kx, ky, kz):
        own = green_matrix((signed[kx], signed[ky], kz))
        if kz in (0, 8):
            own = (own + green_matrix((signed[-kx % 16], signed[-ky % 16], kz))) / 2
        return own

    green = np.zeros((9, len(entry_pairs), 256))
    double = np.array([1, 1, 1, 2, 2, 2])
    for kx in range(9):
        for lane, (ky, kz, kind) in enumerate(modes):
            matrix = green_at(kx, ky, kz) / double[None, :]
            green[kx, :, lane] = [matrix[pair] for pair in entry_pairs]
    green /= table_scale**4 * VOX
    return (
        forward_x,
        inverse_x,
        rounded(first),
        rounded(second),
        rounded((first * weight).T),
        rounded((second * weight).T),
        green.astype(np.float32),
    )


def dot(a, b, dims=((1,), (0,)), precision=None):
    return lax.dot_general(a, b, (dims, ((), ())), precision=precision, preferred_element_type=f32)


def exact_dot(a, b, dims=((1,), (0,))):
    return dot(a, b, dims, lax.Precision.HIGHEST)


def strain_law(s):
    trace = lam_hat * (s[0] + s[1] + s[2])
    return [2.0 * mu_hat * s[k] + trace if k < 3 else 2.0 * mu_hat * s[k] for k in range(6)]


def strain_energy(s):
    return s[0] * s[0] + s[1] * s[1] + s[2] * s[2] + 2.0 * (s[3] * s[3] + s[4] * s[4] + s[5] * s[5])


def cell_kernel(
    count_ref,
    disp_ref,
    below_ref,
    modulus_ref,
    points_ref,
    damage_ref,
    voxel_ref,
    forward_x_ref,
    inverse_x_ref,
    first_ref,
    second_ref,
    first_back_ref,
    second_back_ref,
    green_ref,
    strain_ref,
    force_ref,
    spread_ref,
    own_ref,
    low_ref,
    new_ref,
    nodes_ref,
    macro_ref,
    total_ref,
    polar_ref,
    cos_ref,
    sin_ref,
    spec_cos_ref,
    spec_sin_ref,
    green_cos_ref,
    green_sin_ref,
    plane_ref,
    field_ref,
):
    count = count_ref[0]
    nodes_ref[...] = jnp.zeros(nodes_ref.shape, f32)
    for i in range(3):
        nodes_ref[i, 0:LAYERS, 0:NODES] = disp_ref[i]
        nodes_ref[i, LAYERS : LAYERS + 1, 0:NODES] = below_ref[i]
    rolled = []
    for i in range(3):
        rows = nodes_ref[i]
        for shift in shifts:
            rolled.append(rows if shift == 0 else pltpu.roll(rows, WIDE - shift, 1))
    strain = exact_dot(strain_ref[...], jnp.concatenate(rolled, axis=0))
    points = points_ref[...]
    gauss = points // (LAYERS * EXY * EXY)
    layer = points // (EXY * EXY) % LAYERS
    lane = points % (EXY * EXY) // EXY * ROW + points % EXY
    lane_no = lax.broadcasted_iota(jnp.int32, (WIDE, SLOTS), 0)
    where_at = [
        ((lane_no == lane) & (layer == z)).astype(f32).astype(bf16) for z in range(LAYERS)
    ]
    gauss_no = lax.broadcasted_iota(jnp.int32, (8, SLOTS), 0)
    is_gauss = gauss_no == gauss
    picked = sum(dot(strain[z * 48 : z * 48 + 48].astype(bf16), where_at[z]) for z in range(LAYERS))
    for k in range(6):
        mine = jnp.where(is_gauss, picked[k * 8 : k * 8 + 8], 0.0).astype(bf16)
        macro_ref[k] = dot(mine, jnp.ones((8, 128), bf16), ((0,), (0,)))

    new_ref[...] = damage_ref[...]

    def solve(block):
        base = pl.multiple_of(block * GROUP, GROUP)
        cells = pl.ds(base, GROUP)

        def tiles():
            for x in range(CELL):
                for half in range(2):
                    at = pl.ds(x * 256 + half * 128, 128)
                    rows = pl.ds(x * GROUP, GROUP)
                    lanes = pl.ds(half * 128, 128)
                    yield at, rows, lanes

        def forward(parts):
            for k in range(parts):
                both = dot(forward_x_ref[...], polar_ref[k]).astype(bf16)
                cos_ref[k] = both[: 9 * GROUP]
                sin_ref[k] = both[9 * GROUP :]
            shape_cos, shape_sin = (parts * 9 * GROUP, 256), (parts * 7 * GROUP, 256)
            spec_cos_ref[0:parts] = dot(
                cos_ref[0:parts].reshape(shape_cos), first_ref[...]
            ).reshape(parts, 9 * GROUP, 256)
            spec_sin_ref[0:parts] = dot(
                sin_ref[0:parts].reshape(shape_sin), second_ref[...]
            ).reshape(parts, 7 * GROUP, 256)

        def green_rows(load_cos, load_sin):
            for half in range(2):
                lanes = pl.ds(half * 128, 128)
                for kx in range(9):
                    table = {}
                    for entry, (k, m) in enumerate(entry_pairs):
                        if kx == 0 and odd_in_x[k] != odd_in_x[m]:
                            continue
                        table[k, m] = table[m, k] = green_ref[kx, entry : entry + 1, lanes]

                    def apply(v):
                        return [
                            sum(table[k, m] * v[m] for m in range(6) if (k, m) in table)
                            for k in range(6)
                        ]

                    rows = pl.ds(kx * GROUP, GROUP)
                    a = load_cos(rows, lanes)
                    if kx in (0, 8):
                        a = apply(a)
                        for k in range(6):
                            green_cos_ref[k, rows, lanes] = a[k].astype(bf16)
                        continue
                    rows_sin = pl.ds((kx - 1) * GROUP, GROUP)
                    c = load_sin(rows_sin, lanes)
                    one = apply([c[k] if odd_in_x[k] else a[k] for k in range(6)])
                    two = apply([a[k] if odd_in_x[k] else c[k] for k in range(6)])
                    for k in range(6):
                        cos_part, sin_part = (two, one) if odd_in_x[k] else (one, two)
                        green_cos_ref[k, rows, lanes] = cos_part[k].astype(bf16)
                        green_sin_ref[k, rows_sin, lanes] = sin_part[k].astype(bf16)

        def backward():
            plane_ref[:, 0 : 9 * GROUP] = (
                dot(green_cos_ref[...].reshape(54 * GROUP, 256), first_back_ref[...])
                .astype(bf16)
                .reshape(6, 9 * GROUP, 256)
            )
            plane_ref[:, 9 * GROUP :] = (
                dot(green_sin_ref[...].reshape(42 * GROUP, 256), second_back_ref[...])
                .astype(bf16)
                .reshape(6, 7 * GROUP, 256)
            )
            for k in range(6):
                field_ref[k] = dot(inverse_x_ref[...], plane_ref[k])

        macro = [macro_ref[k, cells, :] for k in range(6)]
        energy = strain_energy(macro)
        uniform = energy / (energy + kappa_sq)
        for at, rows, lanes in tiles():
            old = damage_ref[cells, at].astype(f32)
            young = voxel_ref[cells, at].astype(f32)
            excess = (1.0 - jnp.maximum(old, uniform)) * young - ref_modulus
            polar_ref[0, rows, lanes] = excess.astype(bf16)
        forward(1)
        inner = strain_law(macro)
        inner = [inner[k] if k < 3 else 2.0 * inner[k] for k in range(6)]

        def scaled(ref):
            def load(rows, lanes):
                value = ref[0, rows, lanes]
                return [value * inner[k] for k in range(6)]

            return load

        green_rows(scaled(spec_cos_ref), scaled(spec_sin_ref))
        backward()
        for at, rows, lanes in tiles():
            s = [macro[k] - field_ref[k, rows, lanes] for k in range(6)]
            old = damage_ref[cells, at].astype(f32)
            young = voxel_ref[cells, at].astype(f32)
            energy = strain_energy(s)
            now = jnp.maximum(old, energy / (energy + kappa_sq))
            excess = (1.0 - now) * young - ref_modulus
            polar = strain_law(s)
            for k in range(6):
                value = polar[k] * excess
                polar_ref[k, rows, lanes] = (value if k < 3 else 2.0 * value).astype(bf16)
        forward(6)

        def plain(ref):
            return lambda rows, lanes: [ref[k, rows, lanes] for k in range(6)]

        green_rows(plain(spec_cos_ref), plain(spec_sin_ref))
        backward()
        slot_no = lax.broadcasted_iota(jnp.int32, (GROUP, 128), 0) + base
        live = slot_no < count
        sums = [jnp.zeros((GROUP, 128), f32) for k in range(6)]
        for at, rows, lanes in tiles():
            s = [macro[k] - field_ref[k, rows, lanes] for k in range(6)]
            old = damage_ref[cells, at].astype(f32)
            young = voxel_ref[cells, at].astype(f32)
            energy = strain_energy(s)
            now = jnp.maximum(old, energy / (energy + kappa_sq))
            kept = (1.0 - now) * young
            sums = [sums[k] + kept * s[k] for k in range(6)]
            new_ref[cells, at] = jnp.where(live, now, old).astype(bf16)
        for k in range(6):
            total_ref[k, cells, :] = sums[k]

    lax.fori_loop(0, (count + GROUP - 1) // GROUP, lambda i, c: (solve(i), c)[1], 0)

    slot_live = lax.broadcasted_iota(jnp.int32, (8, SLOTS), 1) < count
    at_point = is_gauss & slot_live
    mean = [
        exact_dot(jnp.ones((8, 128), f32), total_ref[k], ((1,), (1,))) * (1.0 / VOX)
        for k in range(6)
    ]
    cell_stress = [
        jnp.where(at_point, value, 0.0).astype(bf16).astype(f32) for value in strain_law(mean)
    ]
    cell_stress.append(at_point.astype(f32))
    cell_stress = jnp.concatenate(cell_stress, axis=0).astype(bf16)
    stress = []
    for z in range(LAYERS):
        compact = modulus_ref[:, z * 256 : z * 256 + 256]
        young = exact_dot(compact, spread_ref[...])
        from_cells = dot(cell_stress, where_at[z], ((1,), (1,)))
        from_cell = from_cells[48:56] > 0.5
        elastic = strain_law([strain[z * 48 + k * 8 : z * 48 + k * 8 + 8] for k in range(6)])
        for k in range(6):
            stress.append(jnp.where(from_cell, from_cells[k * 8 : k * 8 + 8], young * elastic[k]))
    forces = exact_dot(force_ref[...], jnp.concatenate(stress, axis=0))
    for i in range(3):
        total = 0.0
        for corner, shift in enumerate(shifts):
            part = forces[(i * 4 + corner) * 8 : (i * 4 + corner) * 8 + 8]
            total = total + (part if shift == 0 else pltpu.roll(part, shift, 1))
        own_ref[i] = total[0:LAYERS, 0:NODES]
        low_ref[i] = total[LAYERS : LAYERS + 1, 0:NODES]


def partition_step(displacement, below, modulus, count, points, damage, voxel, interpret=False):
    tables = spectral_tables()
    strain, force = macro_tables()
    operands = [
        displacement,
        below,
        modulus,
        points,
        damage,
        voxel,
        *[jnp.asarray(table) for table in tables],
        jnp.asarray(strain),
        jnp.asarray(force),
        jnp.asarray(spread_table()),
    ]
    vmem = pl.BlockSpec(memory_space=pltpu.VMEM)
    return pl.pallas_call(
        cell_kernel,
        in_specs=[pl.BlockSpec(memory_space=pltpu.SMEM)] + [vmem] * len(operands),
        out_specs=[vmem] * 3,
        out_shape=[
            jax.ShapeDtypeStruct((3, LAYERS, NODES), f32),
            jax.ShapeDtypeStruct((3, 1, NODES), f32),
            jax.ShapeDtypeStruct((SLOTS, VOX), bf16),
        ],
        scratch_shapes=[
            pltpu.VMEM((3, 8, WIDE), f32),
            pltpu.VMEM((6, SLOTS, 128), f32),
            pltpu.VMEM((6, SLOTS, 128), f32),
            pltpu.VMEM((6, 256, 256), bf16),
            pltpu.VMEM((6, 9 * GROUP, 256), bf16),
            pltpu.VMEM((6, 7 * GROUP, 256), bf16),
            pltpu.VMEM((6, 9 * GROUP, 256), f32),
            pltpu.VMEM((6, 7 * GROUP, 256), f32),
            pltpu.VMEM((6, 9 * GROUP, 256), bf16),
            pltpu.VMEM((6, 7 * GROUP, 256), bf16),
            pltpu.VMEM((6, 256, 256), bf16),
            pltpu.VMEM((6, 256, 256), f32),
        ],
        compiler_params=pltpu.CompilerParams(vmem_limit_bytes=48 * 1024 * 1024),
        interpret=interpret,
        name="pier_step",
    )(count, *operands)


def shifted(value, steps):
    axes = ("dom", "sub")
    total = lax.axis_size(axes)
    pairs = [(i, i + steps) for i in range(total) if 0 <= i + steps < total]
    return lax.ppermute(value, axes, pairs)


def body(displacement, modulus, count, points, damage, voxel):
    below = shifted(displacement[:, LAYERS - 1 :], 1)
    own, low, new_damage = partition_step(
        displacement, below, modulus, count, points, damage, voxel
    )
    above = shifted(low, -1)
    return own.at[:, LAYERS - 1 :].add(above), new_damage


def solution(mesh):
    return jax.shard_map(
        body,
        mesh=mesh,
        in_specs=(
            P(None, ("dom", "sub"), None),
            P(None, ("dom", "sub")),
            P(("dom", "sub")),
            P(("dom", "sub"), None),
            P(("dom", "sub"), None),
            P(("dom", "sub"), None),
        ),
        out_specs=(P(None, ("dom", "sub"), None), P(("dom", "sub"), None)),
        check_vma=False,
    )
```

```python
import math

import jax
import jax.numpy as jnp
import ml_dtypes
import numpy as np
from jax import lax
from jax.experimental import pallas as pl
from jax.experimental.pallas import tpu as pltpu
from jax.sharding import PartitionSpec as P

CELL = 16
EXY = 16
VOX = 4096
SLOTS = 64
GROUP = 16
LAYERS = 4
NODES = 289
WIDE = 384
ROW = EXY + 1

lam_hat = 0.2 / 0.72
mu_hat = 1.0 / 2.4
ref_modulus = 2.0
kappa_sq = 4.0
voigt_pairs = ((0, 0), (1, 1), (2, 2), (1, 2), (0, 2), (0, 1))
odd_in_x = (False, False, False, False, True, True)
table_scale = 1.132805
entry_pairs = [(k, m) for k in range(6) for m in range(k, 6)]
f32 = jnp.float32
bf16 = jnp.bfloat16
shifts = (0, 1, ROW, ROW + 1)


def shape_table():
    gauss_coord = 1.0 / math.sqrt(3.0)
    gradients = np.zeros((8, 8, 3), np.float32)
    for corner in range(8):
        signs = [2 * (corner >> d & 1) - 1 for d in range(3)]
        for gauss_no in range(8):
            coords = [(2 * (gauss_no >> d & 1) - 1) * gauss_coord for d in range(3)]
            factor = [(1.0 + signs[d] * coords[d]) / 2.0 for d in range(3)]
            for direction in range(3):
                value = float(signs[direction])
                for other in range(3):
                    if other != direction:
                        value = value * factor[other]
                gradients[corner, gauss_no, direction] = value
    return gradients


def macro_tables():
    gradients = shape_table().astype(np.float64)
    strain = np.zeros((LAYERS, 6, 8, 3, 4, 8))
    force = np.zeros((3, 4, 8, LAYERS, 6, 8))
    for layer in range(LAYERS):
        for corner in range(8):
            node_layer = layer + (corner >> 2)
            row = 4 if node_layer == 0 else node_layer - 1
            shift = corner & 3
            for k, (a, b) in enumerate(voigt_pairs):
                strain[layer, k, :, a, shift, row] += 0.5 * gradients[corner, :, b]
                strain[layer, k, :, b, shift, row] += 0.5 * gradients[corner, :, a]
                force[a, shift, row, layer, k, :] += 0.125 * gradients[corner, :, b]
                if a != b:
                    force[b, shift, row, layer, k, :] += 0.125 * gradients[corner, :, a]
    return (
        strain.reshape(LAYERS * 48, 96).astype(np.float32),
        force.reshape(96, LAYERS * 48).astype(np.float32),
    )


def spread_table():
    table = np.zeros((EXY * EXY, WIDE), np.float32)
    for y in range(EXY):
        for x in range(EXY):
            table[y * EXY + x, y * ROW + x] = 1.0
    return table


def green_matrix(n):
    n = np.asarray(n, np.float64)
    m = n @ n
    out = np.zeros((6, 6))
    if m == 0:
        return out
    lam_ref, mu_ref = ref_modulus * lam_hat, ref_modulus * mu_hat
    coupling = (lam_ref + mu_ref) / (mu_ref * (lam_ref + 2.0 * mu_ref))
    for col, (a, b) in enumerate(voigt_pairs):
        t = np.zeros((3, 3))
        t[a, b] = t[b, a] = 1.0
        u = t @ n
        amp = u / (mu_ref * m) - coupling * (n @ u) * n / m**2
        for k, (c, d) in enumerate(voigt_pairs):
            out[k, col] = 0.5 * (n[c] * amp[d] + n[d] * amp[c])
    return out


def lane_modes():
    modes = []
    for kz in range(1, 8):
        for ky in range(16):
            modes += [(ky, kz, 0), (ky, kz, 1)]
    for kz in (0, 8):
        for ky in range(1, 8):
            modes += [(ky, kz, 0), (ky, kz, 1)]
        modes += [(0, kz, 2), (8, kz, 2)]
    return modes


def spectral_tables():
    side = np.arange(16)
    modes = lane_modes()
    y, z = side.repeat(16), np.tile(side, 16)
    first = np.zeros((256, 256))
    second = np.zeros((256, 256))
    weight = np.zeros(256)
    for lane, (ky, kz, kind) in enumerate(modes):
        phase = 2 * np.pi * ((y * ky + z * kz) % 16) / 16
        first[:, lane] = np.sin(phase) if kind == 1 else np.cos(phase)
        second[:, lane] = (-np.sin(phase), np.cos(phase), np.cos(phase))[kind]
        weight[lane] = 1.0 if kind == 2 else 2.0
    rows = np.zeros((16, 16))
    row_weight = np.full(16, 2.0)
    row_weight[[0, 8]] = 1.0
    for row in range(16):
        k = row if row < 9 else row - 8
        phase = 2 * np.pi * (side * k % 16) / 16
        rows[row] = np.cos(phase) if row < 9 else np.sin(phase)

    def rounded(table):
        table = np.where(np.abs(table) < 1e-9, 0.0, table)
        return (table * table_scale).astype(ml_dtypes.bfloat16)

    eye = np.eye(GROUP)
    forward_x = rounded(np.kron(rows, eye))
    inverse_x = rounded(np.kron((rows * row_weight[:, None]).T, eye))
    signed = np.where(side < 8, side, side - 16)

    def green_at(kx, ky, kz):
        own = green_matrix((signed[kx], signed[ky], kz))
        if kz in (0, 8):
            own = (own + green_matrix((signed[-kx % 16], signed[-ky % 16], kz))) / 2
        return own

    green = np.zeros((9, len(entry_pairs), 256))
    double = np.array([1, 1, 1, 2, 2, 2])
    for kx in range(9):
        for lane, (ky, kz, kind) in enumerate(modes):
            matrix = green_at(kx, ky, kz) / double[None, :]
            green[kx, :, lane] = [matrix[pair] for pair in entry_pairs]
    green /= table_scale**4 * VOX
    return (
        forward_x,
        inverse_x,
        rounded(first),
        rounded(second),
        rounded((first * weight).T),
        rounded((second * weight).T),
        green.astype(np.float32),
    )


def dot(a, b, dims=((1,), (0,)), precision=None):
    return lax.dot_general(a, b, (dims, ((), ())), precision=precision, preferred_element_type=f32)


def split(value, parts):
    out = []
    for _ in range(parts):
        out.append(value.astype(bf16))
        value = value - out[-1].astype(f32)
    return out


def table_split(table, order):
    parts, rest = [], table.astype(np.float64)
    for _ in range(3):
        parts.append(rest.astype(ml_dtypes.bfloat16))
        rest = rest - parts[-1].astype(np.float64)
    return np.concatenate([parts[i] for i in order], axis=1)


def split_dot(table, value, order):
    parts = split(value, max(order) + 1)
    return dot(table, jnp.concatenate([parts[i] for i in order], axis=0))


fine_table, fine_value = (0, 0, 1, 0, 1, 2), (0, 1, 0, 2, 1, 0)
half_table, half_value = (0, 1, 0), (0, 0, 1)


def strain_law(s):
    trace = lam_hat * (s[0] + s[1] + s[2])
    return [2.0 * mu_hat * s[k] + trace if k < 3 else 2.0 * mu_hat * s[k] for k in range(6)]


def strain_energy(s):
    return s[0] * s[0] + s[1] * s[1] + s[2] * s[2] + 2.0 * (s[3] * s[3] + s[4] * s[4] + s[5] * s[5])


def cell_kernel(
    count_ref,
    disp_hbm,
    below_hbm,
    modulus_hbm,
    points_hbm,
    damage_hbm,
    voxel_hbm,
    matrix_hbm,
    green_hbm,
    strain_hbm,
    force_hbm,
    spread_hbm,
    own_ref,
    low_ref,
    new_hbm,
    disp_ref,
    below_ref,
    modulus_ref,
    points_ref,
    damage_ref,
    voxel_ref,
    matrix_ref,
    green_ref,
    strain_ref,
    force_ref,
    spread_ref,
    in_sems,
    out_sems,
    new_ref,
    nodes_ref,
    macro_ref,
    total_ref,
    polar_ref,
    cos_ref,
    sin_ref,
    spec_cos_ref,
    spec_sin_ref,
    green_cos_ref,
    green_sin_ref,
    plane_ref,
    field_ref,
):
    count = count_ref[0]
    pairs = [
        (disp_hbm, disp_ref),
        (below_hbm, below_ref),
        (strain_hbm, strain_ref),
        (points_hbm, points_ref),
        (damage_hbm, damage_ref),
        (voxel_hbm, voxel_ref),
        (matrix_hbm, matrix_ref),
        (green_hbm, green_ref),
        (modulus_hbm, modulus_ref),
        (spread_hbm, spread_ref),
        (force_hbm, force_ref),
    ]
    copies = [
        pltpu.make_async_copy(source, target, in_sems.at[i])
        for i, (source, target) in enumerate(pairs)
    ]
    for copy in copies:
        copy.start()
    forward_x_ref, inverse_x_ref, first_ref, second_ref, first_back_ref, second_back_ref = [
        matrix_ref.at[i] for i in range(6)
    ]
    nodes_ref[...] = jnp.zeros(nodes_ref.shape, f32)
    for copy in copies[:4]:
        copy.wait()
    for i in range(3):
        nodes_ref[i, 0:LAYERS, 0:NODES] = disp_ref[i]
        nodes_ref[i, LAYERS : LAYERS + 1, 0:NODES] = below_ref[i, LAYERS - 1 : LAYERS]
    rolled = []
    for i in range(3):
        rows = nodes_ref[i]
        for shift in shifts:
            rolled.append(rows if shift == 0 else pltpu.roll(rows, WIDE - shift, 1))
    strain = split_dot(strain_ref[...], jnp.concatenate(rolled, axis=0), fine_value)
    points = points_ref[...]
    gauss = points // (LAYERS * EXY * EXY)
    layer = points // (EXY * EXY) % LAYERS
    lane = points % (EXY * EXY) // EXY * ROW + points % EXY
    lane_no = lax.broadcasted_iota(jnp.int32, (WIDE, SLOTS), 0)
    where_at = [
        ((lane_no == lane) & (layer == z)).astype(f32).astype(bf16) for z in range(LAYERS)
    ]
    gauss_no = lax.broadcasted_iota(jnp.int32, (8, SLOTS), 0)
    is_gauss = gauss_no == gauss
    picked = sum(dot(strain[z * 48 : z * 48 + 48].astype(bf16), where_at[z]) for z in range(LAYERS))
    for k in range(6):
        mine = jnp.where(is_gauss, picked[k * 8 : k * 8 + 8], 0.0).astype(bf16)
        macro_ref[k] = dot(mine, jnp.ones((8, 128), bf16), ((0,), (0,)))

    for copy in copies[4:8]:
        copy.wait()

    def store(block, source):
        cells = pl.ds(pl.multiple_of(block * GROUP, GROUP), GROUP)
        return pltpu.make_async_copy(source.at[cells], new_hbm.at[cells], out_sems.at[block])

    def solve(block):
        base = pl.multiple_of(block * GROUP, GROUP)
        cells = pl.ds(base, GROUP)

        def tiles():
            for x in range(CELL):
                for half in range(2):
                    at = pl.ds(x * 256 + half * 128, 128)
                    rows = pl.ds(x * GROUP, GROUP)
                    lanes = pl.ds(half * 128, 128)
                    yield at, rows, lanes

        def forward(parts):
            for k in range(parts):
                both = dot(forward_x_ref[...], polar_ref[k]).astype(bf16)
                cos_ref[k] = both[: 9 * GROUP]
                sin_ref[k] = both[9 * GROUP :]
            shape_cos, shape_sin = (parts * 9 * GROUP, 256), (parts * 7 * GROUP, 256)
            spec_cos_ref[0:parts] = dot(
                cos_ref[0:parts].reshape(shape_cos), first_ref[...]
            ).reshape(parts, 9 * GROUP, 256)
            spec_sin_ref[0:parts] = dot(
                sin_ref[0:parts].reshape(shape_sin), second_ref[...]
            ).reshape(parts, 7 * GROUP, 256)

        def green_rows(load_cos, load_sin):
            for half in range(2):
                lanes = pl.ds(half * 128, 128)
                for kx in range(9):
                    table = {}
                    for entry, (k, m) in enumerate(entry_pairs):
                        if kx == 0 and odd_in_x[k] != odd_in_x[m]:
                            continue
                        table[k, m] = table[m, k] = green_ref[kx, entry : entry + 1, lanes]

                    def apply(v):
                        return [
                            sum(table[k, m] * v[m] for m in range(6) if (k, m) in table)
                            for k in range(6)
                        ]

                    rows = pl.ds(kx * GROUP, GROUP)
                    a = load_cos(rows, lanes)
                    if kx in (0, 8):
                        a = apply(a)
                        for k in range(6):
                            green_cos_ref[k, rows, lanes] = a[k].astype(bf16)
                        continue
                    rows_sin = pl.ds((kx - 1) * GROUP, GROUP)
                    c = load_sin(rows_sin, lanes)
                    one = apply([c[k] if odd_in_x[k] else a[k] for k in range(6)])
                    two = apply([a[k] if odd_in_x[k] else c[k] for k in range(6)])
                    for k in range(6):
                        cos_part, sin_part = (two, one) if odd_in_x[k] else (one, two)
                        green_cos_ref[k, rows, lanes] = cos_part[k].astype(bf16)
                        green_sin_ref[k, rows_sin, lanes] = sin_part[k].astype(bf16)

        def backward():
            plane_ref[:, 0 : 9 * GROUP] = (
                dot(green_cos_ref[...].reshape(54 * GROUP, 256), first_back_ref[...])
                .astype(bf16)
                .reshape(6, 9 * GROUP, 256)
            )
            plane_ref[:, 9 * GROUP :] = (
                dot(green_sin_ref[...].reshape(42 * GROUP, 256), second_back_ref[...])
                .astype(bf16)
                .reshape(6, 7 * GROUP, 256)
            )
            for k in range(6):
                field_ref[k] = dot(inverse_x_ref[...], plane_ref[k])

        macro = [macro_ref[k, cells, :] for k in range(6)]
        energy = strain_energy(macro)
        uniform = energy / (energy + kappa_sq)
        for at, rows, lanes in tiles():
            old = damage_ref[cells, at].astype(f32)
            young = voxel_ref[cells, at].astype(f32)
            excess = (1.0 - jnp.maximum(old, uniform)) * young - ref_modulus
            polar_ref[0, rows, lanes] = excess.astype(bf16)
        forward(1)
        inner = strain_law(macro)
        inner = [inner[k] if k < 3 else 2.0 * inner[k] for k in range(6)]

        def scaled(ref):
            def load(rows, lanes):
                value = ref[0, rows, lanes]
                return [value * inner[k] for k in range(6)]

            return load

        green_rows(scaled(spec_cos_ref), scaled(spec_sin_ref))
        backward()
        for at, rows, lanes in tiles():
            s = [macro[k] - field_ref[k, rows, lanes] for k in range(6)]
            old = damage_ref[cells, at].astype(f32)
            young = voxel_ref[cells, at].astype(f32)
            energy = strain_energy(s)
            now = jnp.maximum(old, energy / (energy + kappa_sq))
            excess = (1.0 - now) * young - ref_modulus
            polar = strain_law(s)
            for k in range(6):
                value = polar[k] * excess
                polar_ref[k, rows, lanes] = (value if k < 3 else 2.0 * value).astype(bf16)
        forward(6)

        def plain(ref):
            return lambda rows, lanes: [ref[k, rows, lanes] for k in range(6)]

        green_rows(plain(spec_cos_ref), plain(spec_sin_ref))
        backward()
        slot_no = lax.broadcasted_iota(jnp.int32, (GROUP, 128), 0) + base
        live = slot_no < count
        sums = [jnp.zeros((GROUP, 128), f32) for k in range(6)]
        for at, rows, lanes in tiles():
            s = [macro[k] - field_ref[k, rows, lanes] for k in range(6)]
            old = damage_ref[cells, at].astype(f32)
            young = voxel_ref[cells, at].astype(f32)
            energy = strain_energy(s)
            now = jnp.maximum(old, energy / (energy + kappa_sq))
            kept = (1.0 - now) * young
            sums = [sums[k] + kept * s[k] for k in range(6)]
            new_ref[cells, at] = jnp.where(live, now, old).astype(bf16)
        for k in range(6):
            total_ref[k, cells, :] = sums[k]

    busy = (count + GROUP - 1) // GROUP

    @pl.loop(busy, SLOTS // GROUP)
    def _(block):
        store(block, damage_ref).start()

    @pl.loop(0, busy)
    def _(block):
        solve(block)
        store(block, new_ref).start()

    for copy in copies[8:]:
        copy.wait()

    slot_live = lax.broadcasted_iota(jnp.int32, (8, SLOTS), 1) < count
    at_point = is_gauss & slot_live
    ones = jnp.ones((8, 384), bf16)
    mean = [
        dot(ones, jnp.concatenate(split(total_ref[k], 3), axis=1), ((1,), (1,))) * (1.0 / VOX)
        for k in range(6)
    ]
    cell_stress = [
        jnp.where(at_point, value, 0.0).astype(bf16).astype(f32) for value in strain_law(mean)
    ]
    cell_stress.append(at_point.astype(f32))
    cell_stress = jnp.concatenate(cell_stress, axis=0).astype(bf16)
    compact = [modulus_ref[:, z * 256 : z * 256 + 256] for z in range(LAYERS)]
    young_parts = dot(jnp.concatenate(split(jnp.concatenate(compact, axis=0), 3), axis=0), spread_ref[...])
    young_all = young_parts[0:32] + young_parts[32:64] + young_parts[64:96]
    stress = []
    for z in range(LAYERS):
        young = young_all[z * 8 : z * 8 + 8]
        from_cells = dot(cell_stress, where_at[z], ((1,), (1,)))
        from_cell = from_cells[48:56] > 0.5
        elastic = strain_law([strain[z * 48 + k * 8 : z * 48 + k * 8 + 8] for k in range(6)])
        for k in range(6):
            stress.append(jnp.where(from_cell, from_cells[k * 8 : k * 8 + 8], young * elastic[k]))
    forces = split_dot(force_ref[...], jnp.concatenate(stress, axis=0), half_value)
    for i in range(3):
        total = 0.0
        for corner, shift in enumerate(shifts):
            part = forces[(i * 4 + corner) * 8 : (i * 4 + corner) * 8 + 8]
            total = total + (part if shift == 0 else pltpu.roll(part, shift, 1))
        own_ref[i] = total[0:LAYERS, 0:NODES]
        low_ref[i, 0 : LAYERS - 1] = jnp.zeros((LAYERS - 1, NODES), f32)
        low_ref[i, LAYERS - 1 : LAYERS] = total[LAYERS : LAYERS + 1, 0:NODES]

    @pl.loop(0, SLOTS // GROUP)
    def _(block):
        store(block, new_ref).wait()


def partition_step(displacement, below, modulus, count, points, damage, voxel):
    *matrices, green = spectral_tables()
    strain, force = macro_tables()
    operands = [
        displacement,
        below,
        modulus,
        points,
        damage,
        voxel,
        jnp.asarray(np.stack(matrices)),
        jnp.asarray(green),
        jnp.asarray(table_split(strain, fine_table)),
        jnp.asarray(table_split(force, half_table)),
        jnp.asarray(spread_table().astype(ml_dtypes.bfloat16)),
    ]
    anywhere = pl.BlockSpec(memory_space=pl.ANY)
    shape = (3, LAYERS, NODES)
    return pl.pallas_call(
        cell_kernel,
        in_specs=[pl.BlockSpec(memory_space=pltpu.SMEM)] + [anywhere] * len(operands),
        out_specs=[pl.BlockSpec(shape), pl.BlockSpec(shape), anywhere],
        out_shape=[
            jax.ShapeDtypeStruct(shape, f32),
            jax.ShapeDtypeStruct(shape, f32),
            jax.ShapeDtypeStruct((SLOTS, VOX), bf16),
        ],
        scratch_shapes=[pltpu.VMEM(x.shape, x.dtype) for x in operands]
        + [
            pltpu.SemaphoreType.DMA((len(operands),)),
            pltpu.SemaphoreType.DMA((SLOTS // GROUP,)),
            pltpu.VMEM((SLOTS, VOX), bf16),
            pltpu.VMEM((3, 8, WIDE), f32),
            pltpu.VMEM((6, SLOTS, 128), f32),
            pltpu.VMEM((6, SLOTS, 128), f32),
            pltpu.VMEM((6, 256, 256), bf16),
            pltpu.VMEM((6, 9 * GROUP, 256), bf16),
            pltpu.VMEM((6, 7 * GROUP, 256), bf16),
            pltpu.VMEM((6, 9 * GROUP, 256), f32),
            pltpu.VMEM((6, 7 * GROUP, 256), f32),
            pltpu.VMEM((6, 9 * GROUP, 256), bf16),
            pltpu.VMEM((6, 7 * GROUP, 256), bf16),
            pltpu.VMEM((6, 256, 256), bf16),
            pltpu.VMEM((6, 256, 256), f32),
        ],
        compiler_params=pltpu.CompilerParams(vmem_limit_bytes=48 * 1024 * 1024),
        name="pier_step",
    )(count, *operands)


def shifted(value, steps):
    axes = ("dom", "sub")
    total = lax.axis_size(axes)
    pairs = [(i, i + steps) for i in range(total) if 0 <= i + steps < total]
    return lax.ppermute(value, axes, pairs)


def body(displacement, modulus, count, points, damage, voxel):
    below = shifted(displacement, 1)
    own, low, new_damage = partition_step(
        displacement, below, modulus, count, points, damage, voxel
    )
    return own + shifted(low, -1), new_damage


def solution(mesh):
    return jax.shard_map(
        body,
        mesh=mesh,
        in_specs=(
            P(None, ("dom", "sub"), None),
            P(None, ("dom", "sub")),
            P(("dom", "sub")),
            P(("dom", "sub"), None),
            P(("dom", "sub"), None),
            P(("dom", "sub"), None),
        ),
        out_specs=(P(None, ("dom", "sub"), None), P(("dom", "sub"), None)),
        check_vma=False,
    )
```

```python
import math

import jax
import jax.numpy as jnp
import ml_dtypes
import numpy as np
from jax import lax
from jax.experimental import pallas as pl
from jax.experimental.pallas import tpu as pltpu
from jax.sharding import PartitionSpec as P

CELL = 16
EXY = 16
VOX = 4096
SLOTS = 64
GROUP = 16
LAYERS = 4
NODES = 289
WIDE = 384
ROW = EXY + 1

lam_hat = 0.2 / 0.72
mu_hat = 1.0 / 2.4
ref_modulus = 2.0
kappa_sq = 4.0
voigt_pairs = ((0, 0), (1, 1), (2, 2), (1, 2), (0, 2), (0, 1))
odd_in_x = (False, False, False, False, True, True)
table_scale = 1.132805
entry_pairs = [(k, m) for k in range(6) for m in range(k, 6)]
f32 = jnp.float32
bf16 = jnp.bfloat16
shifts = (0, 1, ROW, ROW + 1)


def shape_table():
    gauss_coord = 1.0 / math.sqrt(3.0)
    gradients = np.zeros((8, 8, 3), np.float32)
    for corner in range(8):
        signs = [2 * (corner >> d & 1) - 1 for d in range(3)]
        for gauss_no in range(8):
            coords = [(2 * (gauss_no >> d & 1) - 1) * gauss_coord for d in range(3)]
            factor = [(1.0 + signs[d] * coords[d]) / 2.0 for d in range(3)]
            for direction in range(3):
                value = float(signs[direction])
                for other in range(3):
                    if other != direction:
                        value = value * factor[other]
                gradients[corner, gauss_no, direction] = value
    return gradients


def macro_tables():
    gradients = shape_table().astype(np.float64)
    strain = np.zeros((LAYERS, 6, 8, 3, 4, 8))
    force = np.zeros((3, 4, 8, LAYERS, 6, 8))
    for layer in range(LAYERS):
        for corner in range(8):
            node_layer = layer + (corner >> 2)
            row = 4 if node_layer == 0 else node_layer - 1
            shift = corner & 3
            for k, (a, b) in enumerate(voigt_pairs):
                strain[layer, k, :, a, shift, row] += 0.5 * gradients[corner, :, b]
                strain[layer, k, :, b, shift, row] += 0.5 * gradients[corner, :, a]
                force[a, shift, row, layer, k, :] += 0.125 * gradients[corner, :, b]
                if a != b:
                    force[b, shift, row, layer, k, :] += 0.125 * gradients[corner, :, a]
    return (
        strain.reshape(LAYERS * 48, 96).astype(np.float32),
        force.reshape(96, LAYERS * 48).astype(np.float32),
    )


def spread_table():
    table = np.zeros((EXY * EXY, WIDE), np.float32)
    for y in range(EXY):
        for x in range(EXY):
            table[y * EXY + x, y * ROW + x] = 1.0
    return table


def green_matrix(n):
    n = np.asarray(n, np.float64)
    m = n @ n
    out = np.zeros((6, 6))
    if m == 0:
        return out
    lam_ref, mu_ref = ref_modulus * lam_hat, ref_modulus * mu_hat
    coupling = (lam_ref + mu_ref) / (mu_ref * (lam_ref + 2.0 * mu_ref))
    for col, (a, b) in enumerate(voigt_pairs):
        t = np.zeros((3, 3))
        t[a, b] = t[b, a] = 1.0
        u = t @ n
        amp = u / (mu_ref * m) - coupling * (n @ u) * n / m**2
        for k, (c, d) in enumerate(voigt_pairs):
            out[k, col] = 0.5 * (n[c] * amp[d] + n[d] * amp[c])
    return out


def lane_modes():
    modes = []
    for kz in range(1, 8):
        for ky in range(16):
            modes += [(ky, kz, 0), (ky, kz, 1)]
    for kz in (0, 8):
        for ky in range(1, 8):
            modes += [(ky, kz, 0), (ky, kz, 1)]
        modes += [(0, kz, 2), (8, kz, 2)]
    return modes


def spectral_tables():
    side = np.arange(16)
    modes = lane_modes()
    y, z = side.repeat(16), np.tile(side, 16)
    first = np.zeros((256, 256))
    second = np.zeros((256, 256))
    weight = np.zeros(256)
    for lane, (ky, kz, kind) in enumerate(modes):
        phase = 2 * np.pi * ((y * ky + z * kz) % 16) / 16
        first[:, lane] = np.sin(phase) if kind == 1 else np.cos(phase)
        second[:, lane] = (-np.sin(phase), np.cos(phase), np.cos(phase))[kind]
        weight[lane] = 1.0 if kind == 2 else 2.0
    rows = np.zeros((16, 16))
    row_weight = np.full(16, 2.0)
    row_weight[[0, 8]] = 1.0
    for row in range(16):
        k = row if row < 9 else row - 8
        phase = 2 * np.pi * (side * k % 16) / 16
        rows[row] = np.cos(phase) if row < 9 else np.sin(phase)

    def rounded(table):
        table = np.where(np.abs(table) < 1e-9, 0.0, table)
        return (table * table_scale).astype(ml_dtypes.bfloat16)

    eye = np.eye(GROUP)
    forward_x = rounded(np.kron(rows, eye))
    inverse_x = rounded(np.kron((rows * row_weight[:, None]).T, eye))
    signed = np.where(side < 8, side, side - 16)

    def green_at(kx, ky, kz):
        own = green_matrix((signed[kx], signed[ky], kz))
        if kz in (0, 8):
            own = (own + green_matrix((signed[-kx % 16], signed[-ky % 16], kz))) / 2
        return own

    green = np.zeros((9, len(entry_pairs), 256))
    double = np.array([1, 1, 1, 2, 2, 2])
    for kx in range(9):
        for lane, (ky, kz, kind) in enumerate(modes):
            matrix = green_at(kx, ky, kz) / double[None, :]
            green[kx, :, lane] = [matrix[pair] for pair in entry_pairs]
    green /= table_scale**4 * VOX
    return (
        forward_x,
        inverse_x,
        rounded(first),
        rounded(second),
        rounded((first * weight).T),
        rounded((second * weight).T),
        green.astype(np.float32),
    )


def dot(a, b, dims=((1,), (0,)), precision=None):
    return lax.dot_general(a, b, (dims, ((), ())), precision=precision, preferred_element_type=f32)


def split(value, parts):
    out = []
    for _ in range(parts):
        out.append(value.astype(bf16))
        value = value - out[-1].astype(f32)
    return out


def table_split(table, order):
    parts, rest = [], table.astype(np.float64)
    for _ in range(3):
        parts.append(rest.astype(ml_dtypes.bfloat16))
        rest = rest - parts[-1].astype(np.float64)
    return np.concatenate([parts[i] for i in order], axis=1)


def split_dot(table, value, order):
    parts = split(value, max(order) + 1)
    return dot(table, jnp.concatenate([parts[i] for i in order], axis=0))


fine_table, fine_value = (0, 0, 1, 0, 1, 2), (0, 1, 0, 2, 1, 0)
half_table, half_value = (0, 1, 0), (0, 0, 1)


def strain_law(s):
    trace = lam_hat * (s[0] + s[1] + s[2])
    return [2.0 * mu_hat * s[k] + trace if k < 3 else 2.0 * mu_hat * s[k] for k in range(6)]


def strain_energy(s):
    return s[0] * s[0] + s[1] * s[1] + s[2] * s[2] + 2.0 * (s[3] * s[3] + s[4] * s[4] + s[5] * s[5])


def cell_kernel(
    count_ref,
    disp_hbm,
    below_hbm,
    modulus_hbm,
    points_hbm,
    damage_hbm,
    voxel_hbm,
    matrix_hbm,
    green_hbm,
    strain_hbm,
    force_hbm,
    spread_hbm,
    own_ref,
    low_ref,
    new_hbm,
    disp_ref,
    below_ref,
    modulus_ref,
    points_ref,
    damage_ref,
    voxel_ref,
    matrix_ref,
    green_ref,
    strain_ref,
    force_ref,
    spread_ref,
    in_sems,
    out_sems,
    new_ref,
    nodes_ref,
    macro_ref,
    total_ref,
    polar_ref,
    cos_ref,
    sin_ref,
    spec_cos_ref,
    spec_sin_ref,
    green_cos_ref,
    green_sin_ref,
    plane_ref,
    field_ref,
):
    count = count_ref[0]
    pairs = [
        (disp_hbm, disp_ref),
        (below_hbm, below_ref),
        (strain_hbm, strain_ref),
        (points_hbm, points_ref),
        (damage_hbm, damage_ref),
        (voxel_hbm, voxel_ref),
        (matrix_hbm, matrix_ref),
        (green_hbm, green_ref),
        (modulus_hbm, modulus_ref),
        (spread_hbm, spread_ref),
        (force_hbm, force_ref),
    ]
    copies = [
        pltpu.make_async_copy(source, target, in_sems.at[i])
        for i, (source, target) in enumerate(pairs)
    ]
    for copy in copies:
        copy.start()
    forward_x_ref, inverse_x_ref, first_ref, second_ref, first_back_ref, second_back_ref = [
        matrix_ref.at[i] for i in range(6)
    ]
    nodes_ref[...] = jnp.zeros(nodes_ref.shape, f32)
    for copy in copies[:4]:
        copy.wait()
    for i in range(3):
        nodes_ref[i, 0:LAYERS, 0:NODES] = disp_ref[i]
        nodes_ref[i, LAYERS : LAYERS + 1, 0:NODES] = below_ref[i, LAYERS - 1 : LAYERS]
    rolled = []
    for i in range(3):
        rows = nodes_ref[i]
        for shift in shifts:
            rolled.append(rows if shift == 0 else pltpu.roll(rows, WIDE - shift, 1))
    strain = split_dot(strain_ref[...], jnp.concatenate(rolled, axis=0), fine_value)
    points = points_ref[...]
    gauss = points // (LAYERS * EXY * EXY)
    layer = points // (EXY * EXY) % LAYERS
    lane = points % (EXY * EXY) // EXY * ROW + points % EXY
    lane_no = lax.broadcasted_iota(jnp.int32, (WIDE, SLOTS), 0)
    where_at = [
        ((lane_no == lane) & (layer == z)).astype(f32).astype(bf16) for z in range(LAYERS)
    ]
    gauss_no = lax.broadcasted_iota(jnp.int32, (8, SLOTS), 0)
    is_gauss = gauss_no == gauss
    picked = sum(dot(strain[z * 48 : z * 48 + 48].astype(bf16), where_at[z]) for z in range(LAYERS))
    for k in range(6):
        mine = jnp.where(is_gauss, picked[k * 8 : k * 8 + 8], 0.0).astype(bf16)
        macro_ref[k] = dot(mine, jnp.ones((8, 128), bf16), ((0,), (0,)))

    for copy in copies[4:8]:
        copy.wait()

    def store(block, source):
        cells = pl.ds(pl.multiple_of(block * GROUP, GROUP), GROUP)
        return pltpu.make_async_copy(source.at[cells], new_hbm.at[cells], out_sems.at[block])

    def solve(block):
        base = pl.multiple_of(block * GROUP, GROUP)
        cells = pl.ds(base, GROUP)

        def tiles():
            for x in range(CELL):
                for half in range(2):
                    at = pl.ds(x * 256 + half * 128, 128)
                    rows = pl.ds(x * GROUP, GROUP)
                    lanes = pl.ds(half * 128, 128)
                    yield at, rows, lanes

        def forward(parts):
            for k in range(parts):
                both = dot(forward_x_ref[...], polar_ref[k]).astype(bf16)
                cos_ref[k] = both[: 9 * GROUP]
                sin_ref[k] = both[9 * GROUP :]
            shape_cos, shape_sin = (parts * 9 * GROUP, 256), (parts * 7 * GROUP, 256)
            spec_cos_ref[0:parts] = dot(
                cos_ref[0:parts].reshape(shape_cos), first_ref[...]
            ).reshape(parts, 9 * GROUP, 256)
            spec_sin_ref[0:parts] = dot(
                sin_ref[0:parts].reshape(shape_sin), second_ref[...]
            ).reshape(parts, 7 * GROUP, 256)

        def green_rows(load_cos, load_sin):
            for half in range(2):
                lanes = pl.ds(half * 128, 128)
                for kx in range(9):
                    table = {}
                    for entry, (k, m) in enumerate(entry_pairs):
                        if kx == 0 and odd_in_x[k] != odd_in_x[m]:
                            continue
                        table[k, m] = table[m, k] = green_ref[kx, entry : entry + 1, lanes]

                    def apply(v):
                        return [
                            sum(table[k, m] * v[m] for m in range(6) if (k, m) in table)
                            for k in range(6)
                        ]

                    rows = pl.ds(kx * GROUP, GROUP)
                    a = load_cos(rows, lanes)
                    if kx in (0, 8):
                        a = apply(a)
                        for k in range(6):
                            green_cos_ref[k, rows, lanes] = a[k].astype(bf16)
                        continue
                    rows_sin = pl.ds((kx - 1) * GROUP, GROUP)
                    c = load_sin(rows_sin, lanes)
                    one = apply([c[k] if odd_in_x[k] else a[k] for k in range(6)])
                    two = apply([a[k] if odd_in_x[k] else c[k] for k in range(6)])
                    for k in range(6):
                        cos_part, sin_part = (two, one) if odd_in_x[k] else (one, two)
                        green_cos_ref[k, rows, lanes] = cos_part[k].astype(bf16)
                        green_sin_ref[k, rows_sin, lanes] = sin_part[k].astype(bf16)

        def backward():
            plane_ref[:, 0 : 9 * GROUP] = (
                dot(green_cos_ref[...].reshape(54 * GROUP, 256), first_back_ref[...])
                .astype(bf16)
                .reshape(6, 9 * GROUP, 256)
            )
            plane_ref[:, 9 * GROUP :] = (
                dot(green_sin_ref[...].reshape(42 * GROUP, 256), second_back_ref[...])
                .astype(bf16)
                .reshape(6, 7 * GROUP, 256)
            )
            for k in range(6):
                field_ref[k] = dot(inverse_x_ref[...], plane_ref[k])

        macro = [macro_ref[k, cells, :] for k in range(6)]
        energy = strain_energy(macro)
        uniform = energy / (energy + kappa_sq)
        for at, rows, lanes in tiles():
            old = damage_ref[cells, at].astype(f32)
            young = voxel_ref[cells, at].astype(f32)
            excess = (1.0 - jnp.maximum(old, uniform)) * young - ref_modulus
            polar_ref[0, rows, lanes] = excess.astype(bf16)
        forward(1)
        inner = strain_law(macro)
        inner = [inner[k] if k < 3 else 2.0 * inner[k] for k in range(6)]

        def scaled(ref):
            def load(rows, lanes):
                value = ref[0, rows, lanes]
                return [value * inner[k] for k in range(6)]

            return load

        green_rows(scaled(spec_cos_ref), scaled(spec_sin_ref))
        backward()
        for at, rows, lanes in tiles():
            s = [macro[k] - field_ref[k, rows, lanes] for k in range(6)]
            old = damage_ref[cells, at].astype(f32)
            young = voxel_ref[cells, at].astype(f32)
            energy = strain_energy(s)
            now = jnp.maximum(old, energy / (energy + kappa_sq))
            excess = (1.0 - now) * young - ref_modulus
            polar = strain_law(s)
            for k in range(6):
                value = polar[k] * excess
                polar_ref[k, rows, lanes] = (value if k < 3 else 2.0 * value).astype(bf16)
        forward(6)

        def plain(ref):
            return lambda rows, lanes: [ref[k, rows, lanes] for k in range(6)]

        green_rows(plain(spec_cos_ref), plain(spec_sin_ref))
        backward()
        slot_no = lax.broadcasted_iota(jnp.int32, (GROUP, 128), 0) + base
        live = slot_no < count
        sums = [jnp.zeros((GROUP, 128), f32) for k in range(6)]
        for at, rows, lanes in tiles():
            s = [macro[k] - field_ref[k, rows, lanes] for k in range(6)]
            old = damage_ref[cells, at].astype(f32)
            young = voxel_ref[cells, at].astype(f32)
            energy = strain_energy(s)
            now = jnp.maximum(old, energy / (energy + kappa_sq))
            kept = (1.0 - now) * young
            sums = [sums[k] + kept * s[k] for k in range(6)]
            new_ref[cells, at] = jnp.where(live, now, old).astype(bf16)
        for k in range(6):
            total_ref[k, cells, :] = sums[k]

    busy = (count + GROUP - 1) // GROUP

    @pl.loop(busy, SLOTS // GROUP)
    def _(block):
        store(block, damage_ref).start()

    @pl.loop(0, busy)
    def _(block):
        solve(block)
        store(block, new_ref).start()

    for copy in copies[8:]:
        copy.wait()

    slot_live = lax.broadcasted_iota(jnp.int32, (8, SLOTS), 1) < count
    at_point = is_gauss & slot_live
    ones = jnp.ones((8, 384), bf16)
    mean = [
        dot(ones, jnp.concatenate(split(total_ref[k], 3), axis=1), ((1,), (1,))) * (1.0 / VOX)
        for k in range(6)
    ]
    cell_stress = [
        jnp.where(at_point, value, 0.0).astype(bf16).astype(f32) for value in strain_law(mean)
    ]
    cell_stress.append(at_point.astype(f32))
    cell_stress = jnp.concatenate(cell_stress, axis=0).astype(bf16)
    compact = [modulus_ref[:, z * 256 : z * 256 + 256] for z in range(LAYERS)]
    young_parts = dot(jnp.concatenate(split(jnp.concatenate(compact, axis=0), 3), axis=0), spread_ref[...])
    young_all = young_parts[0:32] + young_parts[32:64] + young_parts[64:96]
    stress = []
    for z in range(LAYERS):
        young = young_all[z * 8 : z * 8 + 8]
        from_cells = dot(cell_stress, where_at[z], ((1,), (1,)))
        from_cell = from_cells[48:56] > 0.5
        elastic = strain_law([strain[z * 48 + k * 8 : z * 48 + k * 8 + 8] for k in range(6)])
        for k in range(6):
            stress.append(jnp.where(from_cell, from_cells[k * 8 : k * 8 + 8], young * elastic[k]))
    forces = split_dot(force_ref[...], jnp.concatenate(stress, axis=0), half_value)
    for i in range(3):
        total = 0.0
        for corner, shift in enumerate(shifts):
            part = forces[(i * 4 + corner) * 8 : (i * 4 + corner) * 8 + 8]
            total = total + (part if shift == 0 else pltpu.roll(part, shift, 1))
        own_ref[i] = total[0:LAYERS, 0:NODES]
        low_ref[i, 0 : LAYERS - 1] = jnp.zeros((LAYERS - 1, NODES), f32)
        low_ref[i, LAYERS - 1 : LAYERS] = total[LAYERS : LAYERS + 1, 0:NODES]

    @pl.loop(0, SLOTS // GROUP)
    def _(block):
        store(block, new_ref).wait()


def partition_step(displacement, below, modulus, count, points, damage, voxel):
    *matrices, green = spectral_tables()
    strain, force = macro_tables()
    operands = [
        displacement,
        below,
        modulus,
        points,
        damage,
        voxel,
        jnp.asarray(np.stack(matrices)),
        jnp.asarray(green),
        jnp.asarray(table_split(strain, fine_table)),
        jnp.asarray(table_split(force, half_table)),
        jnp.asarray(spread_table().astype(ml_dtypes.bfloat16)),
    ]
    in_hbm = pl.BlockSpec(memory_space=pltpu.HBM)
    shape = (3, LAYERS, NODES)
    return pl.pallas_call(
        cell_kernel,
        in_specs=[pl.BlockSpec(memory_space=pltpu.SMEM)] + [in_hbm] * len(operands),
        out_specs=[pl.BlockSpec(shape), pl.BlockSpec(shape), in_hbm],
        out_shape=[
            jax.ShapeDtypeStruct(shape, f32),
            jax.ShapeDtypeStruct(shape, f32),
            jax.ShapeDtypeStruct((SLOTS, VOX), bf16),
        ],
        scratch_shapes=[pltpu.VMEM(x.shape, x.dtype) for x in operands]
        + [
            pltpu.SemaphoreType.DMA((len(operands),)),
            pltpu.SemaphoreType.DMA((SLOTS // GROUP,)),
            pltpu.VMEM((SLOTS, VOX), bf16),
            pltpu.VMEM((3, 8, WIDE), f32),
            pltpu.VMEM((6, SLOTS, 128), f32),
            pltpu.VMEM((6, SLOTS, 128), f32),
            pltpu.VMEM((6, 256, 256), bf16),
            pltpu.VMEM((6, 9 * GROUP, 256), bf16),
            pltpu.VMEM((6, 7 * GROUP, 256), bf16),
            pltpu.VMEM((6, 9 * GROUP, 256), f32),
            pltpu.VMEM((6, 7 * GROUP, 256), f32),
            pltpu.VMEM((6, 9 * GROUP, 256), bf16),
            pltpu.VMEM((6, 7 * GROUP, 256), bf16),
            pltpu.VMEM((6, 256, 256), bf16),
            pltpu.VMEM((6, 256, 256), f32),
        ],
        compiler_params=pltpu.CompilerParams(vmem_limit_bytes=64 * 1024 * 1024),
        name="pier_step",
    )(count, *operands)


def shifted(value, steps):
    axes = ("dom", "sub")
    total = lax.axis_size(axes)
    pairs = [(i, i + steps) for i in range(total) if 0 <= i + steps < total]
    return lax.ppermute(value, axes, pairs)


def body(displacement, modulus, count, points, damage, voxel):
    below = shifted(displacement, 1)
    own, low, new_damage = partition_step(
        displacement, below, modulus, count, points, damage, voxel
    )
    return own + shifted(low, -1), new_damage


def solution(mesh):
    return jax.shard_map(
        body,
        mesh=mesh,
        in_specs=(
            P(None, ("dom", "sub"), None),
            P(None, ("dom", "sub")),
            P(("dom", "sub")),
            P(("dom", "sub"), None),
            P(("dom", "sub"), None),
            P(("dom", "sub"), None),
        ),
        out_specs=(P(None, ("dom", "sub"), None), P(("dom", "sub"), None)),
        check_vma=False,
    )
```

```python
import math

import jax
import jax.numpy as jnp
import ml_dtypes
import numpy as np
from jax import lax
from jax.experimental import pallas as pl
from jax.experimental.pallas import tpu as pltpu
from jax.sharding import PartitionSpec as P

CELL = 16
EXY = 16
VOX = 4096
SLOTS = 64
GROUP = 16
LAYERS = 4
NODES = 289
WIDE = 384
ROW = EXY + 1
LAG = 1000

lam_hat = 0.2 / 0.72
mu_hat = 1.0 / 2.4
ref_modulus = 2.0
kappa_sq = 4.0
law_ratio = lam_hat / (2.0 * mu_hat)
voigt_pairs = ((0, 0), (1, 1), (2, 2), (1, 2), (0, 2), (0, 1))
odd_in_x = (False, False, False, False, True, True)
table_scale = 1.132805
entry_pairs = [(k, m) for k in range(6) for m in range(k, 6)]
f32 = jnp.float32
bf16 = jnp.bfloat16
shifts = (0, 1, ROW, ROW + 1)


def shape_table():
    gauss_coord = 1.0 / math.sqrt(3.0)
    gradients = np.zeros((8, 8, 3), np.float32)
    for corner in range(8):
        signs = [2 * (corner >> d & 1) - 1 for d in range(3)]
        for gauss_no in range(8):
            coords = [(2 * (gauss_no >> d & 1) - 1) * gauss_coord for d in range(3)]
            factor = [(1.0 + signs[d] * coords[d]) / 2.0 for d in range(3)]
            for direction in range(3):
                value = float(signs[direction])
                for other in range(3):
                    if other != direction:
                        value = value * factor[other]
                gradients[corner, gauss_no, direction] = value
    return gradients


def macro_tables():
    gradients = shape_table().astype(np.float64)
    strain = np.zeros((LAYERS, 6, 8, 3, 4, 8))
    force = np.zeros((3, 4, 8, LAYERS, 6, 8))
    for layer in range(LAYERS):
        for corner in range(8):
            node_layer = layer + (corner >> 2)
            row = 4 if node_layer == 0 else node_layer - 1
            shift = corner & 3
            for k, (a, b) in enumerate(voigt_pairs):
                strain[layer, k, :, a, shift, row] += 0.5 * gradients[corner, :, b]
                strain[layer, k, :, b, shift, row] += 0.5 * gradients[corner, :, a]
                force[a, shift, row, layer, k, :] += 0.125 * gradients[corner, :, b]
                if a != b:
                    force[b, shift, row, layer, k, :] += 0.125 * gradients[corner, :, a]
    return (
        strain.reshape(LAYERS * 48, 96).astype(np.float32),
        force.reshape(96, LAYERS * 48).astype(np.float32),
    )


def spread_table():
    table = np.zeros((EXY * EXY, WIDE), np.float32)
    for y in range(EXY):
        for x in range(EXY):
            table[y * EXY + x, y * ROW + x] = 1.0
    return table


def green_matrix(n):
    n = np.asarray(n, np.float64)
    m = n @ n
    out = np.zeros((6, 6))
    if m == 0:
        return out
    lam_ref, mu_ref = ref_modulus * lam_hat, ref_modulus * mu_hat
    coupling = (lam_ref + mu_ref) / (mu_ref * (lam_ref + 2.0 * mu_ref))
    for col, (a, b) in enumerate(voigt_pairs):
        t = np.zeros((3, 3))
        t[a, b] = t[b, a] = 1.0
        u = t @ n
        amp = u / (mu_ref * m) - coupling * (n @ u) * n / m**2
        for k, (c, d) in enumerate(voigt_pairs):
            out[k, col] = 0.5 * (n[c] * amp[d] + n[d] * amp[c])
    return out


def lane_modes():
    modes = []
    for kz in range(1, 8):
        for ky in range(16):
            modes += [(ky, kz, 0), (ky, kz, 1)]
    for kz in (0, 8):
        for ky in range(1, 8):
            modes += [(ky, kz, 0), (ky, kz, 1)]
        modes += [(0, kz, 2), (8, kz, 2)]
    return modes


def spectral_tables():
    side = np.arange(16)
    modes = lane_modes()
    y, z = side.repeat(16), np.tile(side, 16)
    first = np.zeros((256, 256))
    second = np.zeros((256, 256))
    weight = np.zeros(256)
    for lane, (ky, kz, kind) in enumerate(modes):
        phase = 2 * np.pi * ((y * ky + z * kz) % 16) / 16
        first[:, lane] = np.sin(phase) if kind == 1 else np.cos(phase)
        second[:, lane] = (-np.sin(phase), np.cos(phase), np.cos(phase))[kind]
        weight[lane] = 1.0 if kind == 2 else 2.0
    rows = np.zeros((16, 16))
    row_weight = np.full(16, 2.0)
    row_weight[[0, 8]] = 1.0
    for row in range(16):
        k = row if row < 9 else row - 8
        phase = 2 * np.pi * (side * k % 16) / 16
        rows[row] = np.cos(phase) if row < 9 else np.sin(phase)

    def rounded(table):
        table = np.where(np.abs(table) < 1e-9, 0.0, table)
        return (table * table_scale).astype(ml_dtypes.bfloat16)

    eye = np.eye(GROUP)
    forward_x = rounded(np.kron(rows, eye))
    inverse_x = rounded(np.kron((rows * row_weight[:, None]).T, eye))
    signed = np.where(side < 8, side, side - 16)

    def green_at(kx, ky, kz):
        own = green_matrix((signed[kx], signed[ky], kz))
        if kz in (0, 8):
            own = (own + green_matrix((signed[-kx % 16], signed[-ky % 16], kz))) / 2
        return own

    green = np.zeros((9, len(entry_pairs), 256))
    double = np.array([1, 1, 1, 2, 2, 2])
    for kx in range(9):
        for lane, (ky, kz, kind) in enumerate(modes):
            matrix = green_at(kx, ky, kz) / double[None, :]
            green[kx, :, lane] = [matrix[pair] for pair in entry_pairs]
    green *= 2.0 * mu_hat / (table_scale**4 * VOX)
    law = np.eye(6)
    law[:3, :3] += law_ratio
    uniform = np.zeros((16, 16, 6, 256))
    sign = np.where(np.array(odd_in_x), -1.0, 1.0)
    for row in range(16):
        kx = (0, 8)[row] if row < 2 else row // 2
        for lane, (ky, kz, kind) in enumerate(modes):
            matrix = green_at(kx, ky, kz) * (2.0 * mu_hat / (table_scale**4 * VOX))
            if row >= 2:
                matrix = matrix * (0.5 if row % 2 == 0 else 0.5 * sign)
            uniform[row, 0:6, :, lane] = (matrix @ law).T
    uniform = uniform.reshape(16, 16, 6 * 256)
    upper = uniform.astype(ml_dtypes.bfloat16).astype(np.float64)
    uniform[:, 6:12] = (uniform - upper)[:, 0:6]
    uniform = uniform.astype(ml_dtypes.bfloat16)
    return (
        forward_x,
        inverse_x,
        rounded(first),
        rounded(second),
        rounded((first * weight).T),
        rounded((second * weight).T),
        uniform,
        green.astype(np.float32),
    )


def dot(a, b, dims=((1,), (0,)), precision=None):
    return lax.dot_general(a, b, (dims, ((), ())), precision=precision, preferred_element_type=f32)


def split(value, parts):
    out = []
    for _ in range(parts):
        out.append(value.astype(bf16))
        value = value - out[-1].astype(f32)
    return out


def table_split(table, order):
    parts, rest = [], table.astype(np.float64)
    for _ in range(3):
        parts.append(rest.astype(ml_dtypes.bfloat16))
        rest = rest - parts[-1].astype(np.float64)
    return np.concatenate([parts[i] for i in order], axis=1)


def split_dot(table, value, order):
    parts = split(value, max(order) + 1)
    return dot(table, jnp.concatenate([parts[i] for i in order], axis=0))


fine_table, fine_value = (0, 0, 1, 0, 1, 2), (0, 1, 0, 2, 1, 0)
half_table, half_value = (0, 1, 0), (0, 0, 1)


def strain_law(s):
    trace = lam_hat * (s[0] + s[1] + s[2])
    return [2.0 * mu_hat * s[k] + trace if k < 3 else 2.0 * mu_hat * s[k] for k in range(6)]


def half_energy(s):
    shear = s[3] * s[3] + s[4] * s[4] + s[5] * s[5]
    return s[0] * s[0] + s[1] * s[1] + s[2] * s[2] + (shear + shear)


def cell_kernel(
    count_ref,
    disp_hbm,
    below_hbm,
    modulus_hbm,
    points_hbm,
    damage_hbm,
    voxel_hbm,
    matrix_hbm,
    uniform_hbm,
    green_hbm,
    strain_hbm,
    force_hbm,
    spread_hbm,
    own_ref,
    low_ref,
    new_hbm,
    disp_ref,
    below_ref,
    modulus_ref,
    points_ref,
    damage_ref,
    voxel_ref,
    matrix_ref,
    uniform_ref,
    green_ref,
    strain_ref,
    force_ref,
    spread_ref,
    in_sems,
    out_sems,
    new_ref,
    nodes_ref,
    macro_ref,
    strain_ref_half,
    total_ref,
    polar_refs,
    cos_refs,
    sin_refs,
    spec_cos_refs,
    spec_sin_refs,
    green_cos_refs,
    green_sin_refs,
    plane_refs,
    field_refs,
):
    count = count_ref[0]
    pairs = [
        (disp_hbm, disp_ref),
        (below_hbm, below_ref),
        (strain_hbm, strain_ref),
        (points_hbm, points_ref),
        (damage_hbm, damage_ref),
        (voxel_hbm, voxel_ref),
        (matrix_hbm, matrix_ref),
        (uniform_hbm, uniform_ref),
        (green_hbm, green_ref),
        (modulus_hbm, modulus_ref),
        (spread_hbm, spread_ref),
        (force_hbm, force_ref),
    ]
    copies = [
        pltpu.make_async_copy(source, target, in_sems.at[i])
        for i, (source, target) in enumerate(pairs)
    ]
    for copy in copies:
        copy.start()
    forward_x_ref, inverse_x_ref, first_ref, second_ref, first_back_ref, second_back_ref = [
        matrix_ref.at[i] for i in range(6)
    ]
    nodes_ref[...] = jnp.zeros(nodes_ref.shape, f32)
    for copy in copies[:4]:
        copy.wait()
    for i in range(3):
        nodes_ref[i, 0:LAYERS, 0:NODES] = disp_ref[i]
        nodes_ref[i, LAYERS : LAYERS + 1, 0:NODES] = below_ref[i, LAYERS - 1 : LAYERS]
    rolled = []
    for i in range(3):
        rows = nodes_ref[i]
        for shift in shifts:
            rolled.append(rows if shift == 0 else pltpu.roll(rows, WIDE - shift, 1))
    strain = split_dot(strain_ref[...], jnp.concatenate(rolled, axis=0), fine_value)
    points = points_ref[...]
    gauss = points // (LAYERS * EXY * EXY)
    layer = points // (EXY * EXY) % LAYERS
    lane = points % (EXY * EXY) // EXY * ROW + points % EXY
    lane_no = lax.broadcasted_iota(jnp.int32, (WIDE, SLOTS), 0)
    where_at = [
        ((lane_no == lane) & (layer == z)).astype(f32).astype(bf16) for z in range(LAYERS)
    ]
    gauss_no = lax.broadcasted_iota(jnp.int32, (8, SLOTS), 0)
    is_gauss = gauss_no == gauss
    picked = sum(dot(strain[z * 48 : z * 48 + 48].astype(bf16), where_at[z]) for z in range(LAYERS))
    for k in range(6):
        mine = jnp.where(is_gauss, picked[k * 8 : k * 8 + 8], 0.0).astype(bf16)
        macro_ref[k] = dot(mine, jnp.full((8, 128), 0.5, bf16), ((0,), (0,)))
        columns = lax.broadcasted_iota(jnp.int32, (8, 16), 1)
        halves = jnp.where((columns == k) | (columns == k + 6), 0.5, 0.0).astype(bf16)
        total = dot(mine, halves, ((0,), (0,)))
        both_macro = total if k == 0 else both_macro + total
    strain_ref_half[...] = both_macro.astype(bf16)

    for copy in copies[4:9]:
        copy.wait()

    def store(block, source):
        cells = pl.ds(pl.multiple_of(block * GROUP, GROUP), GROUP)
        return pltpu.make_async_copy(source.at[cells], new_hbm.at[cells], out_sems.at[block])

    def solve(block, side):
        polar_ref, cos_ref, sin_ref = polar_refs.at[side], cos_refs.at[side], sin_refs.at[side]
        spec_cos_ref, spec_sin_ref = spec_cos_refs.at[side], spec_sin_refs.at[side]
        green_cos_ref, green_sin_ref = green_cos_refs.at[side], green_sin_refs.at[side]
        plane_ref, field_ref = plane_refs.at[side], field_refs.at[side]
        base = pl.multiple_of(block * GROUP, GROUP)
        cells = pl.ds(base, GROUP)
        cos_rows, sin_rows = 9 * GROUP, 7 * GROUP

        def tiles():
            for x in range(CELL):
                for half in range(2):
                    at = pl.ds(x * 256 + half * 128, 128)
                    rows = pl.ds(x * GROUP, GROUP)
                    lanes = pl.ds(half * 128, 128)
                    yield at, rows, lanes

        def forward(parts):
            for k in range(parts):
                both = dot(forward_x_ref[...], polar_ref[k]).astype(bf16)
                cos_ref[k] = both[:cos_rows]
                sin_ref[k] = both[cos_rows:]
                yield 110
            step = min(parts, 3)
            for k in range(0, parts, step):
                some = pl.ds(k, step)
                spec_cos_ref[some] = dot(
                    cos_ref[some].reshape(step * cos_rows, 256), first_ref[...]
                ).reshape(step, cos_rows, 256)
                yield 70 * step
                spec_sin_ref[some] = dot(
                    sin_ref[some].reshape(step * sin_rows, 256), second_ref[...]
                ).reshape(step, sin_rows, 256)
                yield 55 * step

        def green_rows():
            for half in range(2):
                lanes = pl.ds(half * 128, 128)
                for kx in range(9):
                    table = {}
                    for entry, (k, m) in enumerate(entry_pairs):
                        if kx == 0 and odd_in_x[k] != odd_in_x[m]:
                            continue
                        table[k, m] = table[m, k] = green_ref[kx, entry : entry + 1, lanes]

                    def apply(v):
                        return [
                            sum(table[k, m] * v[m] for m in range(6) if (k, m) in table)
                            for k in range(6)
                        ]

                    rows = pl.ds(kx * GROUP, GROUP)
                    a = [spec_cos_ref[k, rows, lanes] for k in range(6)]
                    if kx in (0, 8):
                        a = apply(a)
                        for k in range(6):
                            green_cos_ref[k, rows, lanes] = a[k].astype(bf16)
                        yield 35
                        continue
                    rows_sin = pl.ds((kx - 1) * GROUP, GROUP)
                    c = [spec_sin_ref[k, rows_sin, lanes] for k in range(6)]
                    one = apply([c[k] if odd_in_x[k] else a[k] for k in range(6)])
                    two = apply([a[k] if odd_in_x[k] else c[k] for k in range(6)])
                    for k in range(6):
                        cos_part, sin_part = (two, one) if odd_in_x[k] else (one, two)
                        green_cos_ref[k, rows, lanes] = cos_part[k].astype(bf16)
                        green_sin_ref[k, rows_sin, lanes] = sin_part[k].astype(bf16)
                    yield 70

        def backward():
            for k in range(0, 6, 3):
                some = pl.ds(k, 3)
                plane_ref[some, 0:cos_rows] = (
                    dot(green_cos_ref[some].reshape(3 * cos_rows, 256), first_back_ref[...])
                    .astype(bf16)
                    .reshape(3, cos_rows, 256)
                )
                yield 210
                plane_ref[some, cos_rows:] = (
                    dot(green_sin_ref[some].reshape(3 * sin_rows, 256), second_back_ref[...])
                    .astype(bf16)
                    .reshape(3, sin_rows, 256)
                )
                yield 165
            for k in range(6):
                field_ref[k] = dot(inverse_x_ref[...], plane_ref[k])
                yield 110

        macro = [macro_ref[k, cells, :] for k in range(6)]
        whole = 1.0 / (1.0 + half_energy(macro))
        for at, rows, lanes in tiles():
            old = damage_ref[cells, at].astype(f32)
            young = voxel_ref[cells, at].astype(f32)
            excess = jnp.minimum(1.0 - old, whole) * young - ref_modulus
            polar_ref[0, rows, lanes] = excess.astype(bf16)
            yield 4
        yield from forward(1)
        mine = strain_ref_half[cells, :]
        for kx in (0, 8):
            rows = pl.ds(kx * GROUP, GROUP)
            factor = dot(mine, uniform_ref[kx // 8])
            value = spec_cos_ref[0, rows]
            for k in range(6):
                green_cos_ref[k, rows] = (factor[:, k * 256 : k * 256 + 256] * value).astype(bf16)
            yield 16
        for kx in range(1, 8):
            rows, rows_sin = pl.ds(kx * GROUP, GROUP), pl.ds((kx - 1) * GROUP, GROUP)
            a, c = spec_cos_ref[0, rows], spec_sin_ref[0, rows_sin]
            plus, minus = a + c, a - c
            factor_plus = dot(mine, uniform_ref[2 * kx])
            factor_minus = dot(mine, uniform_ref[2 * kx + 1])
            for k in range(6):
                part = slice(k * 256, k * 256 + 256)
                one, two = factor_plus[:, part] * plus, factor_minus[:, part] * minus
                cos_part, sin_part = one + two, one - two
                if odd_in_x[k]:
                    cos_part, sin_part = sin_part, cos_part
                green_cos_ref[k, rows] = cos_part.astype(bf16)
                green_sin_ref[k, rows_sin] = sin_part.astype(bf16)
            yield 32
        yield from backward()
        for at, rows, lanes in tiles():
            s = [macro[k] - field_ref[k, rows, lanes] for k in range(6)]
            old = damage_ref[cells, at].astype(f32)
            young = voxel_ref[cells, at].astype(f32)
            kept = jnp.minimum(1.0 - old, 1.0 / (1.0 + half_energy(s))) * young
            excess = kept - ref_modulus
            double = excess + excess
            trace = law_ratio * (s[0] + s[1] + s[2])
            for k in range(6):
                value = excess * (s[k] + trace) if k < 3 else double * s[k]
                polar_ref[k, rows, lanes] = value.astype(bf16)
            yield 22
        yield from forward(6)

        yield from green_rows()
        yield from backward()
        slot_no = lax.broadcasted_iota(jnp.int32, (GROUP, 128), 0) + base
        live = slot_no < count
        sums = [jnp.zeros((GROUP, 128), f32) for k in range(6)]
        for at, rows, lanes in tiles():
            s = [macro[k] - field_ref[k, rows, lanes] for k in range(6)]
            old = damage_ref[cells, at].astype(f32)
            young = voxel_ref[cells, at].astype(f32)
            energy = half_energy(s)
            now = jnp.maximum(old, energy / (energy + 1.0))
            kept = (1.0 - now) * young
            sums = [sums[k] + kept * s[k] for k in range(6)]
            new_ref[cells, at] = jnp.where(live, now, old).astype(bf16)
            yield 25
        for k in range(6):
            total_ref[k, cells, :] = sums[k]
        yield 0

    def solve_together(first):
        works = [solve(first, 0), solve(first + 1, 1)]
        clocks = [0, LAG]
        while works:
            turn = clocks.index(min(clocks))
            try:
                clocks[turn] += next(works[turn])
            except StopIteration:
                del works[turn], clocks[turn]

    busy = (count + 2 * GROUP - 1) // (2 * GROUP)

    @pl.loop(2 * busy, SLOTS // GROUP)
    def _(block):
        store(block, damage_ref).start()

    @pl.loop(0, busy)
    def _(pair):
        solve_together(2 * pair)
        store(2 * pair, new_ref).start()
        store(2 * pair + 1, new_ref).start()

    for copy in copies[9:]:
        copy.wait()

    slot_live = lax.broadcasted_iota(jnp.int32, (8, SLOTS), 1) < count
    at_point = is_gauss & slot_live
    ones = jnp.ones((8, 384), bf16)
    mean = [
        dot(ones, jnp.concatenate(split(total_ref[k], 3), axis=1), ((1,), (1,))) * (2.0 / VOX)
        for k in range(6)
    ]
    cell_stress = [
        jnp.where(at_point, value, 0.0).astype(bf16).astype(f32) for value in strain_law(mean)
    ]
    cell_stress.append(at_point.astype(f32))
    cell_stress = jnp.concatenate(cell_stress, axis=0).astype(bf16)
    compact = [modulus_ref[:, z * 256 : z * 256 + 256] for z in range(LAYERS)]
    young_parts = dot(jnp.concatenate(split(jnp.concatenate(compact, axis=0), 3), axis=0), spread_ref[...])
    young_all = young_parts[0:32] + young_parts[32:64] + young_parts[64:96]
    stress = []
    for z in range(LAYERS):
        young = young_all[z * 8 : z * 8 + 8]
        from_cells = dot(cell_stress, where_at[z], ((1,), (1,)))
        from_cell = from_cells[48:56] > 0.5
        elastic = strain_law([strain[z * 48 + k * 8 : z * 48 + k * 8 + 8] for k in range(6)])
        for k in range(6):
            stress.append(jnp.where(from_cell, from_cells[k * 8 : k * 8 + 8], young * elastic[k]))
    forces = split_dot(force_ref[...], jnp.concatenate(stress, axis=0), half_value)
    for i in range(3):
        total = 0.0
        for corner, shift in enumerate(shifts):
            part = forces[(i * 4 + corner) * 8 : (i * 4 + corner) * 8 + 8]
            total = total + (part if shift == 0 else pltpu.roll(part, shift, 1))
        own_ref[i] = total[0:LAYERS, 0:NODES]
        low_ref[i, 0 : LAYERS - 1] = jnp.zeros((LAYERS - 1, NODES), f32)
        low_ref[i, LAYERS - 1 : LAYERS] = total[LAYERS : LAYERS + 1, 0:NODES]

    @pl.loop(0, SLOTS // GROUP)
    def _(block):
        store(block, new_ref).wait()


def partition_step(displacement, below, modulus, count, points, damage, voxel):
    *matrices, uniform, green = spectral_tables()
    strain, force = macro_tables()
    operands = [
        displacement,
        below,
        modulus,
        points,
        damage,
        voxel,
        jnp.asarray(np.stack(matrices)),
        jnp.asarray(uniform),
        jnp.asarray(green),
        jnp.asarray(table_split(strain, fine_table)),
        jnp.asarray(table_split(force, half_table)),
        jnp.asarray(spread_table().astype(ml_dtypes.bfloat16)),
    ]
    in_hbm = pl.BlockSpec(memory_space=pltpu.HBM)
    shape = (3, LAYERS, NODES)
    return pl.pallas_call(
        cell_kernel,
        in_specs=[pl.BlockSpec(memory_space=pltpu.SMEM)] + [in_hbm] * len(operands),
        out_specs=[pl.BlockSpec(shape), pl.BlockSpec(shape), in_hbm],
        out_shape=[
            jax.ShapeDtypeStruct(shape, f32),
            jax.ShapeDtypeStruct(shape, f32),
            jax.ShapeDtypeStruct((SLOTS, VOX), bf16),
        ],
        scratch_shapes=[pltpu.VMEM(x.shape, x.dtype) for x in operands]
        + [
            pltpu.SemaphoreType.DMA((len(operands),)),
            pltpu.SemaphoreType.DMA((SLOTS // GROUP,)),
            pltpu.VMEM((SLOTS, VOX), bf16),
            pltpu.VMEM((3, 8, WIDE), f32),
            pltpu.VMEM((6, SLOTS, 128), f32),
            pltpu.VMEM((SLOTS, 16), bf16),
            pltpu.VMEM((6, SLOTS, 128), f32),
            pltpu.VMEM((2, 6, 256, 256), bf16),
            pltpu.VMEM((2, 6, 9 * GROUP, 256), bf16),
            pltpu.VMEM((2, 6, 7 * GROUP, 256), bf16),
            pltpu.VMEM((2, 6, 9 * GROUP, 256), f32),
            pltpu.VMEM((2, 6, 7 * GROUP, 256), f32),
            pltpu.VMEM((2, 6, 9 * GROUP, 256), bf16),
            pltpu.VMEM((2, 6, 7 * GROUP, 256), bf16),
            pltpu.VMEM((2, 6, 256, 256), bf16),
            pltpu.VMEM((2, 6, 256, 256), f32),
        ],
        compiler_params=pltpu.CompilerParams(vmem_limit_bytes=64 * 1024 * 1024),
        name="pier_step",
    )(count, *operands)


def shifted(value, steps):
    axes = ("dom", "sub")
    total = lax.axis_size(axes)
    pairs = [(i, i + steps) for i in range(total) if 0 <= i + steps < total]
    return lax.ppermute(value, axes, pairs)


def body(displacement, modulus, count, points, damage, voxel):
    below = shifted(displacement, 1)
    own, low, new_damage = partition_step(
        displacement, below, modulus, count, points, damage, voxel
    )
    return own + shifted(low, -1), new_damage


def solution(mesh):
    return jax.shard_map(
        body,
        mesh=mesh,
        in_specs=(
            P(None, ("dom", "sub"), None),
            P(None, ("dom", "sub")),
            P(("dom", "sub")),
            P(("dom", "sub"), None),
            P(("dom", "sub"), None),
            P(("dom", "sub"), None),
        ),
        out_specs=(P(None, ("dom", "sub"), None), P(("dom", "sub"), None)),
        check_vma=False,
    )
```

```python
import math

import jax
import jax.numpy as jnp
import ml_dtypes
import numpy as np
from jax import lax
from jax.experimental import pallas as pl
from jax.experimental.pallas import tpu as pltpu
from jax.sharding import PartitionSpec as P

CELL = 16
EXY = 16
VOX = 4096
SLOTS = 64
GROUP = 16
LAYERS = 4
NODES = 289
WIDE = 384
ROW = EXY + 1
PAIR = 2 * GROUP
LAG = 1000
COS, SIN = 9 * GROUP, 7 * GROUP

lam_hat = 0.2 / 0.72
mu_hat = 1.0 / 2.4
ref_modulus = 2.0
kappa_sq = 4.0
law_ratio = lam_hat / (2.0 * mu_hat)
voigt_pairs = ((0, 0), (1, 1), (2, 2), (1, 2), (0, 2), (0, 1))
odd_in_x = (False, False, False, False, True, True)
table_scale = 1.132805
entry_pairs = [(k, m) for k in range(6) for m in range(k, 6)]
f32 = jnp.float32
bf16 = jnp.bfloat16
shifts = (0, 1, ROW, ROW + 1)


def shape_table():
    gauss_coord = 1.0 / math.sqrt(3.0)
    gradients = np.zeros((8, 8, 3), np.float32)
    for corner in range(8):
        signs = [2 * (corner >> d & 1) - 1 for d in range(3)]
        for gauss_no in range(8):
            coords = [(2 * (gauss_no >> d & 1) - 1) * gauss_coord for d in range(3)]
            factor = [(1.0 + signs[d] * coords[d]) / 2.0 for d in range(3)]
            for direction in range(3):
                value = float(signs[direction])
                for other in range(3):
                    if other != direction:
                        value = value * factor[other]
                gradients[corner, gauss_no, direction] = value
    return gradients


def macro_tables():
    gradients = shape_table().astype(np.float64)
    strain = np.zeros((LAYERS, 6, 8, 3, 4, 8))
    force = np.zeros((3, 4, 8, LAYERS, 6, 8))
    for layer in range(LAYERS):
        for corner in range(8):
            node_layer = layer + (corner >> 2)
            row = 4 if node_layer == 0 else node_layer - 1
            shift = corner & 3
            for k, (a, b) in enumerate(voigt_pairs):
                strain[layer, k, :, a, shift, row] += 0.5 * gradients[corner, :, b]
                strain[layer, k, :, b, shift, row] += 0.5 * gradients[corner, :, a]
                force[a, shift, row, layer, k, :] += 0.125 * gradients[corner, :, b]
                if a != b:
                    force[b, shift, row, layer, k, :] += 0.125 * gradients[corner, :, a]
    return (
        strain.reshape(LAYERS * 48, 96).astype(np.float32),
        force.reshape(96, LAYERS * 48).astype(np.float32),
    )


def spread_table():
    table = np.zeros((EXY * EXY, WIDE), np.float32)
    for y in range(EXY):
        for x in range(EXY):
            table[y * EXY + x, y * ROW + x] = 1.0
    return table


def green_matrix(n):
    n = np.asarray(n, np.float64)
    m = n @ n
    out = np.zeros((6, 6))
    if m == 0:
        return out
    lam_ref, mu_ref = ref_modulus * lam_hat, ref_modulus * mu_hat
    coupling = (lam_ref + mu_ref) / (mu_ref * (lam_ref + 2.0 * mu_ref))
    for col, (a, b) in enumerate(voigt_pairs):
        t = np.zeros((3, 3))
        t[a, b] = t[b, a] = 1.0
        u = t @ n
        amp = u / (mu_ref * m) - coupling * (n @ u) * n / m**2
        for k, (c, d) in enumerate(voigt_pairs):
            out[k, col] = 0.5 * (n[c] * amp[d] + n[d] * amp[c])
    return out


def lane_modes():
    modes = []
    for kz in range(1, 8):
        for ky in range(16):
            modes += [(ky, kz, 0), (ky, kz, 1)]
    for kz in (0, 8):
        for ky in range(1, 8):
            modes += [(ky, kz, 0), (ky, kz, 1)]
        modes += [(0, kz, 2), (8, kz, 2)]
    return modes


def spectral_tables():
    side = np.arange(16)
    modes = lane_modes()
    y, z = side.repeat(16), np.tile(side, 16)
    first = np.zeros((256, 256))
    second = np.zeros((256, 256))
    weight = np.zeros(256)
    for lane, (ky, kz, kind) in enumerate(modes):
        phase = 2 * np.pi * ((y * ky + z * kz) % 16) / 16
        first[:, lane] = np.sin(phase) if kind == 1 else np.cos(phase)
        second[:, lane] = (-np.sin(phase), np.cos(phase), np.cos(phase))[kind]
        weight[lane] = 1.0 if kind == 2 else 2.0
    rows = np.zeros((16, 16))
    row_weight = np.full(16, 2.0)
    row_weight[[0, 8]] = 1.0
    for row in range(16):
        k = row if row < 9 else row - 8
        phase = 2 * np.pi * (side * k % 16) / 16
        rows[row] = np.cos(phase) if row < 9 else np.sin(phase)

    def rounded(table):
        table = np.where(np.abs(table) < 1e-9, 0.0, table)
        return (table * table_scale).astype(ml_dtypes.bfloat16)

    eye = np.eye(GROUP)
    forward_x = rounded(np.kron(rows, eye))
    inverse_x = rounded(np.kron((rows * row_weight[:, None]).T, eye))
    signed = np.where(side < 8, side, side - 16)

    def green_at(kx, ky, kz):
        own = green_matrix((signed[kx], signed[ky], kz))
        if kz in (0, 8):
            own = (own + green_matrix((signed[-kx % 16], signed[-ky % 16], kz))) / 2
        return own

    green = np.zeros((9, len(entry_pairs), 256))
    double = np.array([1, 1, 1, 2, 2, 2])
    for kx in range(9):
        for lane, (ky, kz, kind) in enumerate(modes):
            matrix = green_at(kx, ky, kz) / double[None, :]
            green[kx, :, lane] = [matrix[pair] for pair in entry_pairs]
    green *= 2.0 * mu_hat / (table_scale**4 * VOX)
    law = np.eye(6)
    law[:3, :3] += law_ratio
    uniform = np.zeros((16, 16, 6, 256))
    sign = np.where(np.array(odd_in_x), -1.0, 1.0)
    for row in range(16):
        kx = (0, 8)[row] if row < 2 else row // 2
        for lane, (ky, kz, kind) in enumerate(modes):
            matrix = green_at(kx, ky, kz) * (2.0 * mu_hat / (table_scale**4 * VOX))
            if row >= 2:
                matrix = matrix * (0.5 if row % 2 == 0 else 0.5 * sign)
            uniform[row, 0:6, :, lane] = (matrix @ law).T
    uniform = uniform.reshape(16, 16, 6 * 256)
    upper = uniform.astype(ml_dtypes.bfloat16).astype(np.float64)
    uniform[:, 6:12] = (uniform - upper)[:, 0:6]
    uniform = uniform.astype(ml_dtypes.bfloat16)
    return (
        forward_x,
        inverse_x,
        rounded(first),
        rounded(second),
        rounded((first * weight).T),
        rounded((second * weight).T),
        uniform,
        green.astype(np.float32),
    )


def dot(a, b, dims=((1,), (0,)), precision=None):
    return lax.dot_general(a, b, (dims, ((), ())), precision=precision, preferred_element_type=f32)


def split(value, parts):
    out = []
    for _ in range(parts):
        out.append(value.astype(bf16))
        value = value - out[-1].astype(f32)
    return out


def table_split(table, order):
    parts, rest = [], table.astype(np.float64)
    for _ in range(3):
        parts.append(rest.astype(ml_dtypes.bfloat16))
        rest = rest - parts[-1].astype(np.float64)
    return np.concatenate([parts[i] for i in order], axis=1)


def split_dot(table, value, order):
    parts = split(value, max(order) + 1)
    return dot(table, jnp.concatenate([parts[i] for i in order], axis=0))


fine_table, fine_value = (0, 0, 1, 0, 1, 2), (0, 1, 0, 2, 1, 0)
half_table, half_value = (0, 1, 0), (0, 0, 1)


def strain_law(s):
    trace = lam_hat * (s[0] + s[1] + s[2])
    return [2.0 * mu_hat * s[k] + trace if k < 3 else 2.0 * mu_hat * s[k] for k in range(6)]


def half_energy(s):
    shear = s[3] * s[3] + s[4] * s[4] + s[5] * s[5]
    return s[0] * s[0] + s[1] * s[1] + s[2] * s[2] + (shear + shear)


class Cells:
    shared = ("damage", "voxel", "new", "macro", "half", "total", "matrix", "uniform", "table")
    own = ("polar", "cos", "sin", "spec_cos", "spec_sin", "green_cos", "green_sin", "plane", "field")

    def __init__(self, refs, count):
        self.count = count
        refs = list(refs)
        for name in self.shared:
            setattr(self, name, refs.pop(0))
        self.sides = [dict(zip(self.own, refs[side * 9 : side * 9 + 9])) for side in range(2)]

    @staticmethod
    def scratch():
        cos, sin, full = (6, COS, 256), (6, SIN, 256), (6, 256, 256)
        side = [
            pltpu.VMEM(full, bf16),
            pltpu.VMEM(cos, bf16),
            pltpu.VMEM(sin, bf16),
            pltpu.VMEM(cos, bf16),
            pltpu.VMEM(sin, bf16),
            pltpu.VMEM(cos, bf16),
            pltpu.VMEM(sin, bf16),
            pltpu.VMEM(full, bf16),
            pltpu.VMEM(full, f32),
        ]
        return [
            pltpu.VMEM((SLOTS, VOX), bf16),
            pltpu.VMEM((SLOTS, VOX), bf16),
            pltpu.VMEM((SLOTS, VOX), bf16),
            pltpu.VMEM((6, SLOTS, 128), f32),
            pltpu.VMEM((SLOTS, 16), bf16),
            pltpu.VMEM((6, SLOTS, 128), f32),
            pltpu.VMEM((6, 256, 256), bf16),
            pltpu.VMEM((16, 16, 6 * 256), bf16),
            pltpu.VMEM((9, len(entry_pairs), 256), f32),
            *side,
            *side,
        ]

    def solve_pair(self, pair):
        a, b = Group(self, 2 * pair, 0), Group(self, 2 * pair + 1, 1)
        in_turns(a.all_steps(), b.all_steps())


def in_turns(*works):
    works, clocks = list(works), [LAG * i for i in range(len(works))]
    while works:
        turn = clocks.index(min(clocks))
        try:
            clocks[turn] += next(works[turn])
        except StopIteration:
            del works[turn], clocks[turn]


class Group:
    def __init__(self, cells, block, side):
        for name in Cells.shared:
            setattr(self, name, getattr(cells, name))
        for name, ref in cells.sides[side].items():
            setattr(self, name, ref)
        self.cells = pl.ds(pl.multiple_of(block * GROUP, GROUP), GROUP)

    def all_steps(self):
        yield from self.first_field()
        yield from self.first_green()
        yield from self.both(self.back)
        yield from self.back_x()
        yield from self.update()
        yield from self.forward()
        yield from self.both(self.green)
        yield from self.both(self.back)
        yield from self.back_x()
        yield from self.finish()

    def back_x(self):
        for k in range(6):
            self.field[k] = dot(self.matrix[1], self.plane[k])
            yield 110

    def both(self, step):
        for i in range(2):
            yield from step(i)

    def tiles(self):
        for x in range(CELL):
            for half in range(2):
                lanes = pl.ds(half * 128, 128)
                at = pl.ds(x * 256 + half * 128, 128)
                old = self.damage[self.cells, at].astype(f32)
                young = self.voxel[self.cells, at].astype(f32)
                yield old, young, pl.ds(x * GROUP, GROUP), lanes, at

    def to_x_modes(self, k):
        both = dot(self.matrix[0], self.polar[k]).astype(bf16)
        self.cos[k] = both[:COS]
        self.sin[k] = both[COS:]

    def to_lane_modes(self, some, count):
        self.spec_cos[some] = dot(
            self.cos[some].reshape(count * COS, 256), self.matrix[2]
        ).astype(bf16).reshape(count, COS, 256)
        yield 70 * count
        self.spec_sin[some] = dot(
            self.sin[some].reshape(count * SIN, 256), self.matrix[3]
        ).astype(bf16).reshape(count, SIN, 256)
        yield 55 * count

    def first_field(self):
        macro = [self.macro[k, self.cells, :] for k in range(6)]
        whole = 1.0 / (1.0 + half_energy(macro))
        for old, young, rows, lanes, _ in self.tiles():
            excess = jnp.minimum(1.0 - old, whole) * young - ref_modulus
            self.polar[0, rows, lanes] = excess.astype(bf16)
            yield 4
        self.to_x_modes(0)
        yield 110
        yield from self.to_lane_modes(pl.ds(0, 1), 1)

    def first_green(self):
        mine = self.half[self.cells, :]
        for kx in (0, 8):
            rows = pl.ds(kx * GROUP, GROUP)
            factor = dot(mine, self.uniform[kx // 8])
            value = self.spec_cos[0, rows].astype(f32)
            for k in range(6):
                self.green_cos[k, rows] = (factor[:, k * 256 : k * 256 + 256] * value).astype(bf16)
            yield 16
        for kx in range(1, 8):
            rows, rows_sin = pl.ds(kx * GROUP, GROUP), pl.ds((kx - 1) * GROUP, GROUP)
            a, c = self.spec_cos[0, rows].astype(f32), self.spec_sin[0, rows_sin].astype(f32)
            plus, minus = a + c, a - c
            factor_plus = dot(mine, self.uniform[2 * kx])
            factor_minus = dot(mine, self.uniform[2 * kx + 1])
            for k in range(6):
                part = slice(k * 256, k * 256 + 256)
                one, two = factor_plus[:, part] * plus, factor_minus[:, part] * minus
                cos_part, sin_part = one + two, one - two
                if odd_in_x[k]:
                    cos_part, sin_part = sin_part, cos_part
                self.green_cos[k, rows] = cos_part.astype(bf16)
                self.green_sin[k, rows_sin] = sin_part.astype(bf16)
            yield 32

    def back(self, i):
        some = pl.ds(i * 3, 3)
        self.plane[some, 0:COS] = (
            dot(self.green_cos[some].reshape(3 * COS, 256), self.matrix[4])
            .astype(bf16)
            .reshape(3, COS, 256)
        )
        yield 210
        self.plane[some, COS:] = (
            dot(self.green_sin[some].reshape(3 * SIN, 256), self.matrix[5])
            .astype(bf16)
            .reshape(3, SIN, 256)
        )
        yield 165

    def strains(self, rows, lanes):
        return [self.macro[k, self.cells, :] - self.field[k, rows, lanes] for k in range(6)]

    def update(self):
        for old, young, rows, lanes, _ in self.tiles():
            s = self.strains(rows, lanes)
            kept = jnp.minimum(1.0 - old, 1.0 / (1.0 + half_energy(s))) * young
            excess = kept - ref_modulus
            double = excess + excess
            trace = law_ratio * (s[0] + s[1] + s[2])
            for k in range(6):
                value = excess * (s[k] + trace) if k < 3 else double * s[k]
                self.polar[k, rows, lanes] = value.astype(bf16)
            yield 22

    def forward(self):
        for k in range(6):
            self.to_x_modes(k)
            yield 110
        for i in range(2):
            yield from self.to_lane_modes(pl.ds(i * 3, 3), 3)

    def green(self, i):
        lanes = pl.ds(pl.multiple_of(i * 128, 128), 128)
        for kx in range(9):
            table = {}
            for entry, (k, m) in enumerate(entry_pairs):
                if kx == 0 and odd_in_x[k] != odd_in_x[m]:
                    continue
                table[k, m] = table[m, k] = self.table[kx, entry : entry + 1, lanes]

            def apply(v):
                return [
                    sum(table[k, m] * v[m] for m in range(6) if (k, m) in table) for k in range(6)
                ]

            rows = pl.ds(kx * GROUP, GROUP)
            a = [self.spec_cos[k, rows, lanes].astype(f32) for k in range(6)]
            if kx in (0, 8):
                a = apply(a)
                for k in range(6):
                    self.green_cos[k, rows, lanes] = a[k].astype(bf16)
                yield 35
                continue
            rows_sin = pl.ds((kx - 1) * GROUP, GROUP)
            c = [self.spec_sin[k, rows_sin, lanes].astype(f32) for k in range(6)]
            one = apply([c[k] if odd_in_x[k] else a[k] for k in range(6)])
            two = apply([a[k] if odd_in_x[k] else c[k] for k in range(6)])
            for k in range(6):
                cos_part, sin_part = (two, one) if odd_in_x[k] else (one, two)
                self.green_cos[k, rows, lanes] = cos_part[k].astype(bf16)
                self.green_sin[k, rows_sin, lanes] = sin_part[k].astype(bf16)
            yield 70

    def finish(self):
        sums = [jnp.zeros((GROUP, 128), f32) for k in range(6)]
        for old, young, rows, lanes, at in self.tiles():
            s = self.strains(rows, lanes)
            energy = half_energy(s)
            now = jnp.maximum(old, energy / (energy + 1.0))
            kept = (1.0 - now) * young
            sums = [sums[k] + kept * s[k] for k in range(6)]
            self.new[self.cells, at] = now.astype(bf16)
            yield 25
        for k in range(6):
            self.total[k, self.cells, :] = sums[k]
        yield 0


def macro_strain(nodes_ref, strain_ref):
    rolled = []
    for i in range(3):
        rows = nodes_ref[i]
        for shift in shifts:
            rolled.append(rows if shift == 0 else pltpu.roll(rows, WIDE - shift, 1))
    return split_dot(strain_ref[...], jnp.concatenate(rolled, axis=0), fine_value)


def locate(points):
    gauss = points // (LAYERS * EXY * EXY)
    layer = points // (EXY * EXY) % LAYERS
    lane = points % (EXY * EXY) // EXY * ROW + points % EXY
    lane_no = lax.broadcasted_iota(jnp.int32, (WIDE, SLOTS), 0)
    where_at = [
        ((lane_no == lane) & (layer == z)).astype(f32).astype(bf16) for z in range(LAYERS)
    ]
    return where_at, lax.broadcasted_iota(jnp.int32, (8, SLOTS), 0) == gauss


def pick_strains(strain, where_at, is_gauss, macro_ref, half_ref):
    picked = sum(dot(strain[z * 48 : z * 48 + 48].astype(bf16), where_at[z]) for z in range(LAYERS))
    for k in range(6):
        mine = jnp.where(is_gauss, picked[k * 8 : k * 8 + 8], 0.0).astype(bf16)
        macro_ref[k] = dot(mine, jnp.full((8, 128), 0.5, bf16), ((0,), (0,)))
        columns = lax.broadcasted_iota(jnp.int32, (8, 16), 1)
        halves = jnp.where((columns == k) | (columns == k + 6), 0.5, 0.0).astype(bf16)
        total = dot(mine, halves, ((0,), (0,)))
        both = total if k == 0 else both + total
    half_ref[...] = both.astype(bf16)


def start_copies(pairs, sems):
    copies = [
        pltpu.make_async_copy(source, target, sems.at[i])
        for i, (source, target) in enumerate(pairs)
    ]
    for copy in copies:
        copy.start()

    def wait(some):
        for copy in copies[some]:
            copy.wait()

    return wait


def pier_kernel(count_ref, *refs):
    total = len(operand_names)
    sources, refs = refs[:total], refs[total:]
    own_ref, low_ref, new_hbm, *refs = refs
    targets, refs = refs[:7], refs[7:]
    in_sems, out_sems, nodes_ref, *refs = refs
    count = count_ref[0]
    cells = Cells(refs, count)
    disp_ref, below_ref, strain_ref, points_ref = targets[:4]
    modulus_ref, spread_ref, force_ref = targets[4:]
    targets = [
        *targets[:4],
        cells.damage,
        cells.voxel,
        cells.matrix,
        cells.uniform,
        cells.table,
        *targets[4:],
    ]
    wait = start_copies(list(zip(sources, targets, strict=True)), in_sems)
    nodes_ref[...] = jnp.zeros(nodes_ref.shape, f32)
    wait(slice(0, 4))
    for i in range(3):
        nodes_ref[i, 0:LAYERS, 0:NODES] = disp_ref[i]
        nodes_ref[i, LAYERS : LAYERS + 1, 0:NODES] = below_ref[i, LAYERS - 1 : LAYERS]
    where_at, is_gauss = locate(points_ref[...])
    strain = macro_strain(nodes_ref, strain_ref)
    pick_strains(strain, where_at, is_gauss, cells.macro, cells.half)
    wait(slice(4, 9))
    busy = (count + PAIR - 1) // PAIR

    def store(pair, source):
        rows = pl.ds(pl.multiple_of(pair * PAIR, PAIR), PAIR)
        return pltpu.make_async_copy(source.at[rows], new_hbm.at[rows], out_sems.at[pair])

    @pl.loop(busy, SLOTS // PAIR)
    def _(pair):
        store(pair, cells.damage).start()

    @pl.loop(0, busy)
    def _(pair):
        cells.solve_pair(pair)
        rows = pl.ds(pl.multiple_of(pair * PAIR, PAIR), PAIR)
        live = lax.broadcasted_iota(jnp.int32, (PAIR, 128), 0) + pair * PAIR < count

        @pl.when((pair + 1) * PAIR > count)
        def _():
            for start in range(0, VOX, 128):
                lanes = pl.ds(start, 128)
                new, old = cells.new[rows, lanes], cells.damage[rows, lanes]
                new, old = new.astype(f32), old.astype(f32)
                cells.new[rows, lanes] = jnp.where(live, new, old).astype(bf16)

        store(pair, cells.new).start()

    wait(slice(9, total))

    slot_live = lax.broadcasted_iota(jnp.int32, (8, SLOTS), 1) < count
    at_point = is_gauss & slot_live
    ones = jnp.ones((8, 384), bf16)
    mean = [
        dot(ones, jnp.concatenate(split(cells.total[k], 3), axis=1), ((1,), (1,))) * (2.0 / VOX)
        for k in range(6)
    ]
    cell_stress = [
        jnp.where(at_point, value, 0.0).astype(bf16).astype(f32) for value in strain_law(mean)
    ]
    cell_stress.append(at_point.astype(f32))
    cell_stress = jnp.concatenate(cell_stress, axis=0).astype(bf16)
    compact = [modulus_ref[:, z * 256 : z * 256 + 256] for z in range(LAYERS)]
    young_parts = dot(jnp.concatenate(split(jnp.concatenate(compact, axis=0), 3), axis=0), spread_ref[...])
    young_all = young_parts[0:32] + young_parts[32:64] + young_parts[64:96]
    stress = []
    for z in range(LAYERS):
        young = young_all[z * 8 : z * 8 + 8]
        from_cells = dot(cell_stress, where_at[z], ((1,), (1,)))
        from_cell = from_cells[48:56] > 0.5
        elastic = strain_law([strain[z * 48 + k * 8 : z * 48 + k * 8 + 8] for k in range(6)])
        for k in range(6):
            stress.append(jnp.where(from_cell, from_cells[k * 8 : k * 8 + 8], young * elastic[k]))
    forces = split_dot(force_ref[...], jnp.concatenate(stress, axis=0), half_value)
    for i in range(3):
        total = 0.0
        for corner, shift in enumerate(shifts):
            part = forces[(i * 4 + corner) * 8 : (i * 4 + corner) * 8 + 8]
            total = total + (part if shift == 0 else pltpu.roll(part, shift, 1))
        own_ref[i] = total[0:LAYERS, 0:NODES]
        low_ref[i, 0 : LAYERS - 1] = jnp.zeros((LAYERS - 1, NODES), f32)
        low_ref[i, LAYERS - 1 : LAYERS] = total[LAYERS : LAYERS + 1, 0:NODES]


    @pl.loop(0, SLOTS // PAIR)
    def _(pair):
        store(pair, cells.new).wait()


operand_names = (
    *("disp", "below", "strain", "points", "damage", "voxel"),
    *("matrix", "uniform", "green", "modulus", "spread", "force"),
)


def call(kernel, name, count, operands, names, copied, out_specs, out_shape, scratch):
    values = [operands[key] for key in names]
    in_hbm = pl.BlockSpec(memory_space=pltpu.HBM)
    return pl.pallas_call(
        kernel,
        in_specs=[pl.BlockSpec(memory_space=pltpu.SMEM)] + [in_hbm] * len(values),
        out_specs=out_specs,
        out_shape=out_shape,
        scratch_shapes=[pltpu.VMEM(operands[key].shape, operands[key].dtype) for key in copied]
        + [pltpu.SemaphoreType.DMA((len(values),)), pltpu.SemaphoreType.DMA((4,))]
        + scratch
        + [pltpu.VMEM((3, 8, WIDE), f32)]
        + Cells.scratch(),
        compiler_params=pltpu.CompilerParams(vmem_limit_bytes=64 * 1024 * 1024),
        name=name,
    )(count, *values)


def partition_step(displacement, below, modulus, count, points, damage, voxel):
    *matrices, uniform, green = spectral_tables()
    strain, force = macro_tables()
    operands = dict(
        disp=displacement,
        below=below,
        modulus=modulus,
        points=points,
        damage=damage,
        voxel=voxel,
        matrix=jnp.asarray(np.stack(matrices)),
        uniform=jnp.asarray(uniform),
        green=jnp.asarray(green),
        strain=jnp.asarray(table_split(strain, fine_table)),
        force=jnp.asarray(table_split(force, half_table)),
        spread=jnp.asarray(spread_table().astype(ml_dtypes.bfloat16)),
    )
    in_hbm = pl.BlockSpec(memory_space=pltpu.HBM)
    shape = (3, LAYERS, NODES)
    return call(
        pier_kernel,
        "pier_step",
        count,
        operands,
        operand_names,
        operand_names[:4] + operand_names[9:],
        [pl.BlockSpec(shape), pl.BlockSpec(shape), in_hbm],
        [
            jax.ShapeDtypeStruct(shape, f32),
            jax.ShapeDtypeStruct(shape, f32),
            jax.ShapeDtypeStruct((SLOTS, VOX), bf16),
        ],
        [],
    )


def shifted(value, steps):
    axes = ("dom", "sub")
    total = lax.axis_size(axes)
    pairs = [(i, i + steps) for i in range(total) if 0 <= i + steps < total]
    return lax.ppermute(value, axes, pairs)


def body(displacement, modulus, count, points, damage, voxel):
    below = shifted(displacement, 1)
    own, low, new_damage = partition_step(
        displacement, below, modulus, count, points, damage, voxel
    )
    return own + shifted(low, -1), new_damage


def solution(mesh):
    return jax.shard_map(
        body,
        mesh=mesh,
        in_specs=(
            P(None, ("dom", "sub"), None),
            P(None, ("dom", "sub")),
            P(("dom", "sub")),
            P(("dom", "sub"), None),
            P(("dom", "sub"), None),
            P(("dom", "sub"), None),
        ),
        out_specs=(P(None, ("dom", "sub"), None), P(("dom", "sub"), None)),
        check_vma=False,
    )
```

```python
import math

import jax
import jax.numpy as jnp
import ml_dtypes
import numpy as np
from jax import lax
from jax.experimental import pallas as pl
from jax.experimental.pallas import tpu as pltpu
from jax.sharding import PartitionSpec as P

CELL = 16
EXY = 16
VOX = 4096
SLOTS = 64
GROUP = 16
LAYERS = 4
NODES = 289
WIDE = 384
ROW = EXY + 1
PAIR = 2 * GROUP
LAG = 1000
COS, SIN = 9 * GROUP, 7 * GROUP

lam_hat = 0.2 / 0.72
mu_hat = 1.0 / 2.4
ref_modulus = 2.0
kappa_sq = 4.0
law_ratio = lam_hat / (2.0 * mu_hat)
voigt_pairs = ((0, 0), (1, 1), (2, 2), (1, 2), (0, 2), (0, 1))
odd_in_x = (False, False, False, False, True, True)
table_scale = 1.132805
entry_pairs = [(k, m) for k in range(6) for m in range(k, 6)]
f32 = jnp.float32
bf16 = jnp.bfloat16
shifts = (0, 1, ROW, ROW + 1)


def shape_table():
    gauss_coord = 1.0 / math.sqrt(3.0)
    gradients = np.zeros((8, 8, 3), np.float32)
    for corner in range(8):
        signs = [2 * (corner >> d & 1) - 1 for d in range(3)]
        for gauss_no in range(8):
            coords = [(2 * (gauss_no >> d & 1) - 1) * gauss_coord for d in range(3)]
            factor = [(1.0 + signs[d] * coords[d]) / 2.0 for d in range(3)]
            for direction in range(3):
                value = float(signs[direction])
                for other in range(3):
                    if other != direction:
                        value = value * factor[other]
                gradients[corner, gauss_no, direction] = value
    return gradients


def macro_tables():
    gradients = shape_table().astype(np.float64)
    strain = np.zeros((LAYERS, 6, 8, 3, 4, 8))
    force = np.zeros((3, 4, 8, LAYERS, 6, 8))
    for layer in range(LAYERS):
        for corner in range(8):
            node_layer = layer + (corner >> 2)
            row = 4 if node_layer == 0 else node_layer - 1
            shift = corner & 3
            for k, (a, b) in enumerate(voigt_pairs):
                strain[layer, k, :, a, shift, row] += 0.5 * gradients[corner, :, b]
                strain[layer, k, :, b, shift, row] += 0.5 * gradients[corner, :, a]
                force[a, shift, row, layer, k, :] += 0.125 * gradients[corner, :, b]
                if a != b:
                    force[b, shift, row, layer, k, :] += 0.125 * gradients[corner, :, a]
    return (
        strain.reshape(LAYERS * 48, 96).astype(np.float32),
        force.reshape(96, LAYERS * 48).astype(np.float32),
    )


def spread_table():
    table = np.zeros((EXY * EXY, WIDE), np.float32)
    for y in range(EXY):
        for x in range(EXY):
            table[y * EXY + x, y * ROW + x] = 1.0
    return table


def green_matrix(n):
    n = np.asarray(n, np.float64)
    m = n @ n
    out = np.zeros((6, 6))
    if m == 0:
        return out
    lam_ref, mu_ref = ref_modulus * lam_hat, ref_modulus * mu_hat
    coupling = (lam_ref + mu_ref) / (mu_ref * (lam_ref + 2.0 * mu_ref))
    for col, (a, b) in enumerate(voigt_pairs):
        t = np.zeros((3, 3))
        t[a, b] = t[b, a] = 1.0
        u = t @ n
        amp = u / (mu_ref * m) - coupling * (n @ u) * n / m**2
        for k, (c, d) in enumerate(voigt_pairs):
            out[k, col] = 0.5 * (n[c] * amp[d] + n[d] * amp[c])
    return out


def lane_modes():
    modes = []
    for kz in range(1, 8):
        for ky in range(16):
            modes += [(ky, kz, 0), (ky, kz, 1)]
    for kz in (0, 8):
        for ky in range(1, 8):
            modes += [(ky, kz, 0), (ky, kz, 1)]
        modes += [(0, kz, 2), (8, kz, 2)]
    return modes


def spectral_tables():
    side = np.arange(16)
    modes = lane_modes()
    y, z = side.repeat(16), np.tile(side, 16)
    first = np.zeros((256, 256))
    second = np.zeros((256, 256))
    weight = np.zeros(256)
    for lane, (ky, kz, kind) in enumerate(modes):
        phase = 2 * np.pi * ((y * ky + z * kz) % 16) / 16
        first[:, lane] = np.sin(phase) if kind == 1 else np.cos(phase)
        second[:, lane] = (-np.sin(phase), np.cos(phase), np.cos(phase))[kind]
        weight[lane] = 1.0 if kind == 2 else 2.0
    rows = np.zeros((16, 16))
    row_weight = np.full(16, 2.0)
    row_weight[[0, 8]] = 1.0
    for row in range(16):
        k = row if row < 9 else row - 8
        phase = 2 * np.pi * (side * k % 16) / 16
        rows[row] = np.cos(phase) if row < 9 else np.sin(phase)

    def rounded(table):
        table = np.where(np.abs(table) < 1e-9, 0.0, table)
        return (table * table_scale).astype(ml_dtypes.bfloat16)

    eye = np.eye(GROUP)
    forward_x = rounded(np.kron(rows, eye))
    inverse_x = rounded(np.kron((rows * row_weight[:, None]).T, eye))
    signed = np.where(side < 8, side, side - 16)

    def green_at(kx, ky, kz):
        own = green_matrix((signed[kx], signed[ky], kz))
        if kz in (0, 8):
            own = (own + green_matrix((signed[-kx % 16], signed[-ky % 16], kz))) / 2
        return own

    green = np.zeros((9, len(entry_pairs), 256))
    double = np.array([1, 1, 1, 2, 2, 2])
    for kx in range(9):
        for lane, (ky, kz, kind) in enumerate(modes):
            matrix = green_at(kx, ky, kz) / double[None, :]
            green[kx, :, lane] = [matrix[pair] for pair in entry_pairs]
    scale = 2.0 * mu_hat / (table_scale**4 * VOX)
    green *= scale
    lam_ref, mu_ref = ref_modulus * lam_hat, ref_modulus * mu_hat
    coupling = (lam_ref + mu_ref) / (mu_ref * (lam_ref + 2.0 * mu_ref))
    for kx in range(9):
        for lane, (ky, kz, kind) in enumerate(modes[:128]):
            assert 0 < kz < 8
            n = np.array([signed[kx], signed[ky], kz], np.float64)
            n = n / math.sqrt(n @ n) * math.sqrt(scale / mu_ref)
            green[kx, 0:3, lane] = n
            green[kx, 3:6, lane] = n / 2
            green[kx, 6:9, lane] = n * (coupling * mu_ref**2 / scale)
    law = np.eye(6)
    law[:3, :3] += law_ratio
    uniform = np.zeros((16, 16, 6, 256))
    sign = np.where(np.array(odd_in_x), -1.0, 1.0)
    for row in range(16):
        kx = (0, 8)[row] if row < 2 else row // 2
        for lane, (ky, kz, kind) in enumerate(modes):
            matrix = green_at(kx, ky, kz) * (2.0 * mu_hat / (table_scale**4 * VOX))
            if row >= 2:
                matrix = matrix * (0.5 if row % 2 == 0 else 0.5 * sign)
            uniform[row, 0:6, :, lane] = (matrix @ law).T
    uniform = uniform.reshape(16, 16, 6 * 256)
    upper = uniform.astype(ml_dtypes.bfloat16).astype(np.float64)
    uniform[:, 6:12] = (uniform - upper)[:, 0:6]
    uniform = uniform.astype(ml_dtypes.bfloat16)
    return (
        forward_x,
        inverse_x,
        rounded(first),
        rounded(second),
        rounded((first * weight).T),
        rounded((second * weight).T),
        uniform,
        green.astype(np.float32),
    )


def dot(a, b, dims=((1,), (0,)), precision=None):
    return lax.dot_general(a, b, (dims, ((), ())), precision=precision, preferred_element_type=f32)


def split(value, parts):
    out = []
    for _ in range(parts):
        out.append(value.astype(bf16))
        value = value - out[-1].astype(f32)
    return out


def table_split(table, order):
    parts, rest = [], table.astype(np.float64)
    for _ in range(3):
        parts.append(rest.astype(ml_dtypes.bfloat16))
        rest = rest - parts[-1].astype(np.float64)
    return np.concatenate([parts[i] for i in order], axis=1)


def split_dot(table, value, order):
    parts = split(value, max(order) + 1)
    return dot(table, jnp.concatenate([parts[i] for i in order], axis=0))


half_table, half_value = (0, 1, 0), (0, 0, 1)


def strain_law(s):
    trace = lam_hat * (s[0] + s[1] + s[2])
    return [2.0 * mu_hat * s[k] + trace if k < 3 else 2.0 * mu_hat * s[k] for k in range(6)]


def half_energy(s):
    shear = s[3] * s[3] + s[4] * s[4] + s[5] * s[5]
    return s[0] * s[0] + s[1] * s[1] + s[2] * s[2] + (shear + shear)


class Cells:
    shared = ("damage", "voxel", "new", "macro", "half", "total", "matrix", "uniform", "table")
    own = ("polar", "cos", "sin", "spec_cos", "spec_sin", "green_cos", "green_sin", "plane", "field")

    def __init__(self, refs, count):
        self.count = count
        refs = list(refs)
        for name in self.shared:
            setattr(self, name, refs.pop(0))
        self.sides = [dict(zip(self.own, refs[side * 9 : side * 9 + 9])) for side in range(2)]

    @staticmethod
    def scratch():
        cos, sin, full = (6, COS, 256), (6, SIN, 256), (6, 256, 256)
        side = [
            pltpu.VMEM(full, bf16),
            pltpu.VMEM(cos, bf16),
            pltpu.VMEM(sin, bf16),
            pltpu.VMEM(cos, bf16),
            pltpu.VMEM(sin, bf16),
            pltpu.VMEM(cos, bf16),
            pltpu.VMEM(sin, bf16),
            pltpu.VMEM(full, bf16),
            pltpu.VMEM(full, f32),
        ]
        return [
            pltpu.VMEM((SLOTS, VOX), bf16),
            pltpu.VMEM((SLOTS, VOX), bf16),
            pltpu.VMEM((SLOTS, VOX), bf16),
            pltpu.VMEM((6, SLOTS, 128), f32),
            pltpu.VMEM((SLOTS, 16), bf16),
            pltpu.VMEM((6, SLOTS, 128), f32),
            pltpu.VMEM((6, 256, 256), bf16),
            pltpu.VMEM((16, 16, 6 * 256), bf16),
            pltpu.VMEM((9, len(entry_pairs), 256), f32),
            *side,
            *side,
        ]

    def solve_pair(self, pair):
        a, b = Group(self, 2 * pair, 0), Group(self, 2 * pair + 1, 1)
        in_turns(a.all_steps(), b.all_steps())


def in_turns(*works):
    works, clocks = list(works), [LAG * i for i in range(len(works))]
    while works:
        turn = clocks.index(min(clocks))
        try:
            clocks[turn] += next(works[turn])
        except StopIteration:
            del works[turn], clocks[turn]


def by_formula(nx, ny, nz, hx, hy, hz, cx, cy, cz, xx, yy, zz, yz, xz, xy):
    ux = nx * xx + hy * xy + hz * xz
    uy = ny * yy + hx * xy + hz * yz
    uz = nz * zz + hx * xz + hy * yz
    along = nx * ux + ny * uy + nz * uz
    ux, uy, uz = ux - cx * along, uy - cy * along, uz - cz * along
    return [
        *(nx * ux, ny * uy, nz * uz),
        *(hy * uz + hz * uy, hx * uz + hz * ux, hx * uy + hy * ux),
    ]


class Group:
    def __init__(self, cells, block, side):
        for name in Cells.shared:
            setattr(self, name, getattr(cells, name))
        for name, ref in cells.sides[side].items():
            setattr(self, name, ref)
        self.cells = pl.ds(pl.multiple_of(block * GROUP, GROUP), GROUP)

    def all_steps(self):
        yield from self.first_field()
        yield from self.first_green()
        yield from self.both(self.back)
        yield from self.back_x()
        yield from self.update()
        yield from self.forward()
        yield from self.both(self.green)
        yield from self.both(self.back)
        yield from self.back_x()
        yield from self.finish()

    def back_x(self):
        for k in range(6):
            self.field[k] = dot(self.matrix[1], self.plane[k])
            yield 110

    def both(self, step):
        for i in range(2):
            yield from step(i)

    def tiles(self):
        for x in range(CELL):
            for half in range(2):
                lanes = pl.ds(half * 128, 128)
                at = pl.ds(x * 256 + half * 128, 128)
                old = self.damage[self.cells, at].astype(f32)
                young = self.voxel[self.cells, at].astype(f32)
                yield old, young, pl.ds(x * GROUP, GROUP), lanes, at

    def to_x_modes(self, k):
        both = dot(self.matrix[0], self.polar[k]).astype(bf16)
        self.cos[k] = both[:COS]
        self.sin[k] = both[COS:]

    def to_lane_modes(self, some, count):
        self.spec_cos[some] = dot(
            self.cos[some].reshape(count * COS, 256), self.matrix[2]
        ).astype(bf16).reshape(count, COS, 256)
        yield 70 * count
        self.spec_sin[some] = dot(
            self.sin[some].reshape(count * SIN, 256), self.matrix[3]
        ).astype(bf16).reshape(count, SIN, 256)
        yield 55 * count

    def first_field(self):
        macro = [self.macro[k, self.cells, :] for k in range(6)]
        whole = 1.0 / (1.0 + half_energy(macro))
        for old, young, rows, lanes, _ in self.tiles():
            excess = jnp.minimum(1.0 - old, whole) * young - ref_modulus
            self.polar[0, rows, lanes] = excess.astype(bf16)
            yield 4
        self.to_x_modes(0)
        yield 110
        yield from self.to_lane_modes(pl.ds(0, 1), 1)

    def first_green(self):
        mine = self.half[self.cells, :]
        for kx in (0, 8):
            rows = pl.ds(kx * GROUP, GROUP)
            factor = dot(mine, self.uniform[kx // 8])
            value = self.spec_cos[0, rows].astype(f32)
            for k in range(6):
                self.green_cos[k, rows] = (factor[:, k * 256 : k * 256 + 256] * value).astype(bf16)
            yield 16
        for kx in range(1, 8):
            rows, rows_sin = pl.ds(kx * GROUP, GROUP), pl.ds((kx - 1) * GROUP, GROUP)
            a, c = self.spec_cos[0, rows].astype(f32), self.spec_sin[0, rows_sin].astype(f32)
            plus, minus = a + c, a - c
            factor_plus = dot(mine, self.uniform[2 * kx])
            factor_minus = dot(mine, self.uniform[2 * kx + 1])
            for k in range(6):
                part = slice(k * 256, k * 256 + 256)
                one, two = factor_plus[:, part] * plus, factor_minus[:, part] * minus
                cos_part, sin_part = one + two, one - two
                if odd_in_x[k]:
                    cos_part, sin_part = sin_part, cos_part
                self.green_cos[k, rows] = cos_part.astype(bf16)
                self.green_sin[k, rows_sin] = sin_part.astype(bf16)
            yield 32

    def back(self, i):
        some = pl.ds(i * 3, 3)
        self.plane[some, 0:COS] = (
            dot(self.green_cos[some].reshape(3 * COS, 256), self.matrix[4])
            .astype(bf16)
            .reshape(3, COS, 256)
        )
        yield 210
        self.plane[some, COS:] = (
            dot(self.green_sin[some].reshape(3 * SIN, 256), self.matrix[5])
            .astype(bf16)
            .reshape(3, SIN, 256)
        )
        yield 165

    def strains(self, rows, lanes):
        return [self.macro[k, self.cells, :] - self.field[k, rows, lanes] for k in range(6)]

    def update(self):
        for old, young, rows, lanes, _ in self.tiles():
            s = self.strains(rows, lanes)
            kept = jnp.minimum(1.0 - old, 1.0 / (1.0 + half_energy(s))) * young
            excess = kept - ref_modulus
            double = excess + excess
            trace = law_ratio * (s[0] + s[1] + s[2])
            for k in range(6):
                value = excess * (s[k] + trace) if k < 3 else double * s[k]
                self.polar[k, rows, lanes] = value.astype(bf16)
            yield 22

    def forward(self):
        for k in range(6):
            self.to_x_modes(k)
            yield 110
        for i in range(2):
            yield from self.to_lane_modes(pl.ds(i * 3, 3), 3)

    def green(self, i):
        lanes = pl.ds(pl.multiple_of(i * 128, 128), 128)
        for kx in range(9):
            table = {}
            for entry, (k, m) in enumerate(entry_pairs):
                if kx == 0 and odd_in_x[k] != odd_in_x[m]:
                    continue
                table[k, m] = table[m, k] = self.table[kx, entry : entry + 1, lanes]

            def apply(v):
                if i == 0:
                    return by_formula(*[self.table[kx, j : j + 1, lanes] for j in range(9)], *v)
                return [
                    sum(table[k, m] * v[m] for m in range(6) if (k, m) in table) for k in range(6)
                ]

            rows = pl.ds(kx * GROUP, GROUP)
            a = [self.spec_cos[k, rows, lanes].astype(f32) for k in range(6)]
            if kx in (0, 8):
                a = apply(a)
                for k in range(6):
                    self.green_cos[k, rows, lanes] = a[k].astype(bf16)
                yield 35
                continue
            rows_sin = pl.ds((kx - 1) * GROUP, GROUP)
            c = [self.spec_sin[k, rows_sin, lanes].astype(f32) for k in range(6)]
            one = apply([c[k] if odd_in_x[k] else a[k] for k in range(6)])
            two = apply([a[k] if odd_in_x[k] else c[k] for k in range(6)])
            for k in range(6):
                cos_part, sin_part = (two, one) if odd_in_x[k] else (one, two)
                self.green_cos[k, rows, lanes] = cos_part[k].astype(bf16)
                self.green_sin[k, rows_sin, lanes] = sin_part[k].astype(bf16)
            yield 70

    def finish(self):
        sums = [jnp.zeros((GROUP, 128), f32) for k in range(6)]
        for old, young, rows, lanes, at in self.tiles():
            s = self.strains(rows, lanes)
            energy = half_energy(s)
            now = jnp.maximum(old, energy / (energy + 1.0))
            kept = (1.0 - now) * young
            sums = [sums[k] + kept * s[k] for k in range(6)]
            self.new[self.cells, at] = now.astype(bf16)
            yield 25
        for k in range(6):
            self.total[k, self.cells, :] = sums[k]
        yield 0


def macro_strain(nodes_ref, strain_ref):
    rolled = []
    for i in range(3):
        rows = nodes_ref[i]
        for shift in shifts:
            rolled.append(rows if shift == 0 else pltpu.roll(rows, WIDE - shift, 1))
    return split_dot(strain_ref[...], jnp.concatenate(rolled, axis=0), half_value)


def locate(points):
    gauss = points // (LAYERS * EXY * EXY)
    layer = points // (EXY * EXY) % LAYERS
    lane = points % (EXY * EXY) // EXY * ROW + points % EXY
    lane_no = lax.broadcasted_iota(jnp.int32, (WIDE, SLOTS), 0)
    where_at = [
        ((lane_no == lane) & (layer == z)).astype(f32).astype(bf16) for z in range(LAYERS)
    ]
    return where_at, lax.broadcasted_iota(jnp.int32, (8, SLOTS), 0) == gauss


def pick_strains(strain, where_at, is_gauss, macro_ref, half_ref):
    picked = sum(dot(strain[z * 48 : z * 48 + 48].astype(bf16), where_at[z]) for z in range(LAYERS))
    picked = jnp.where(jnp.concatenate([is_gauss] * 6, axis=0), picked, 0.0).astype(bf16)
    rows = lax.broadcasted_iota(jnp.int32, (48, 7 * 128), 0) // 8
    lanes = lax.broadcasted_iota(jnp.int32, (48, 7 * 128), 1)
    spread = jnp.where(lanes < 768, lanes // 128, (lanes - 768) % 6)
    spread = jnp.where((spread == rows) & (lanes < 768 + 12), 0.5, 0.0).astype(bf16)
    out = dot(picked, spread, ((0,), (0,)))
    for k in range(6):
        macro_ref[k] = out[:, k * 128 : k * 128 + 128]
    half_ref[...] = out[:, 768:784].astype(bf16)


def start_copies(pairs, sems):
    copies = [
        pltpu.make_async_copy(source, target, sems.at[i])
        for i, (source, target) in enumerate(pairs)
    ]
    for copy in copies:
        copy.start()

    def wait(some):
        for copy in copies[some]:
            copy.wait()

    return wait


def pier_kernel(count_ref, *refs):
    total = len(operand_names)
    sources, refs = refs[:total], refs[total:]
    own_ref, low_ref, new_hbm, *refs = refs
    targets, refs = refs[:7], refs[7:]
    in_sems, out_sems, nodes_ref, *refs = refs
    count = count_ref[0]
    cells = Cells(refs, count)
    disp_ref, below_ref, strain_ref, points_ref = targets[:4]
    modulus_ref, spread_ref, force_ref = targets[4:]
    targets = [
        *targets[:4],
        cells.damage,
        cells.voxel,
        cells.matrix,
        cells.uniform,
        cells.table,
        *targets[4:],
    ]
    wait = start_copies(list(zip(sources, targets, strict=True)), in_sems)
    nodes_ref[...] = jnp.zeros(nodes_ref.shape, f32)
    wait(slice(0, 4))
    for i in range(3):
        nodes_ref[i, 0:LAYERS, 0:NODES] = disp_ref[i]
        nodes_ref[i, LAYERS : LAYERS + 1, 0:NODES] = below_ref[i, LAYERS - 1 : LAYERS]
    where_at, is_gauss = locate(points_ref[...])
    strain = macro_strain(nodes_ref, strain_ref)
    pick_strains(strain, where_at, is_gauss, cells.macro, cells.half)
    wait(slice(4, 9))
    busy = (count + PAIR - 1) // PAIR

    def store(pair, source):
        rows = pl.ds(pl.multiple_of(pair * PAIR, PAIR), PAIR)
        return pltpu.make_async_copy(source.at[rows], new_hbm.at[rows], out_sems.at[pair])

    @pl.loop(busy, SLOTS // PAIR)
    def _(pair):
        store(pair, cells.damage).start()

    @pl.loop(0, busy)
    def _(pair):
        cells.solve_pair(pair)
        rows = pl.ds(pl.multiple_of(pair * PAIR, PAIR), PAIR)
        live = lax.broadcasted_iota(jnp.int32, (PAIR, 128), 0) + pair * PAIR < count

        @pl.when((pair + 1) * PAIR > count)
        def _():
            for start in range(0, VOX, 128):
                lanes = pl.ds(start, 128)
                new, old = cells.new[rows, lanes], cells.damage[rows, lanes]
                new, old = new.astype(f32), old.astype(f32)
                cells.new[rows, lanes] = jnp.where(live, new, old).astype(bf16)

        store(pair, cells.new).start()

    wait(slice(9, total))

    slot_live = lax.broadcasted_iota(jnp.int32, (8, SLOTS), 1) < count
    at_point = is_gauss & slot_live
    ones = jnp.ones((8, 256), bf16)
    mean = [
        dot(ones, jnp.concatenate(split(cells.total[k], 2), axis=1), ((1,), (1,))) * (2.0 / VOX)
        for k in range(6)
    ]
    cell_stress = [
        jnp.where(at_point, value, 0.0).astype(bf16).astype(f32) for value in strain_law(mean)
    ]
    cell_stress.append(at_point.astype(f32))
    cell_stress = jnp.concatenate(cell_stress, axis=0).astype(bf16)
    compact = [modulus_ref[:, z * 256 : z * 256 + 256] for z in range(LAYERS)]
    young_parts = dot(jnp.concatenate(split(jnp.concatenate(compact, axis=0), 3), axis=0), spread_ref[...])
    young_all = young_parts[0:32] + young_parts[32:64] + young_parts[64:96]
    stress = []
    for z in range(LAYERS):
        young = young_all[z * 8 : z * 8 + 8]
        from_cells = dot(cell_stress, where_at[z], ((1,), (1,)))
        from_cell = from_cells[48:56] > 0.5
        elastic = strain_law([strain[z * 48 + k * 8 : z * 48 + k * 8 + 8] for k in range(6)])
        for k in range(6):
            stress.append(jnp.where(from_cell, from_cells[k * 8 : k * 8 + 8], young * elastic[k]))
    forces = split_dot(force_ref[...], jnp.concatenate(stress, axis=0), half_value)
    for i in range(3):
        total = 0.0
        for corner, shift in enumerate(shifts):
            part = forces[(i * 4 + corner) * 8 : (i * 4 + corner) * 8 + 8]
            total = total + (part if shift == 0 else pltpu.roll(part, shift, 1))
        own_ref[i] = total[0:LAYERS, 0:NODES]
        low_ref[i, 0 : LAYERS - 1] = jnp.zeros((LAYERS - 1, NODES), f32)
        low_ref[i, LAYERS - 1 : LAYERS] = total[LAYERS : LAYERS + 1, 0:NODES]


    @pl.loop(0, SLOTS // PAIR)
    def _(pair):
        store(pair, cells.new).wait()


operand_names = (
    *("disp", "below", "strain", "points", "damage", "voxel"),
    *("matrix", "uniform", "green", "modulus", "spread", "force"),
)


def call(kernel, name, count, operands, names, copied, out_specs, out_shape, scratch):
    values = [operands[key] for key in names]
    in_hbm = pl.BlockSpec(memory_space=pltpu.HBM)
    return pl.pallas_call(
        kernel,
        in_specs=[pl.BlockSpec(memory_space=pltpu.SMEM)] + [in_hbm] * len(values),
        out_specs=out_specs,
        out_shape=out_shape,
        scratch_shapes=[pltpu.VMEM(operands[key].shape, operands[key].dtype) for key in copied]
        + [pltpu.SemaphoreType.DMA((len(values),)), pltpu.SemaphoreType.DMA((4,))]
        + scratch
        + [pltpu.VMEM((3, 8, WIDE), f32)]
        + Cells.scratch(),
        compiler_params=pltpu.CompilerParams(vmem_limit_bytes=64 * 1024 * 1024),
        name=name,
    )(count, *values)


def partition_step(displacement, below, modulus, count, points, damage, voxel):
    *matrices, uniform, green = spectral_tables()
    strain, force = macro_tables()
    operands = dict(
        disp=displacement,
        below=below,
        modulus=modulus,
        points=points,
        damage=damage,
        voxel=voxel,
        matrix=jnp.asarray(np.stack(matrices)),
        uniform=jnp.asarray(uniform),
        green=jnp.asarray(green),
        strain=jnp.asarray(table_split(strain, half_table)),
        force=jnp.asarray(table_split(force, half_table)),
        spread=jnp.asarray(spread_table().astype(ml_dtypes.bfloat16)),
    )
    in_hbm = pl.BlockSpec(memory_space=pltpu.HBM)
    shape = (3, LAYERS, NODES)
    return call(
        pier_kernel,
        "pier_step",
        count,
        operands,
        operand_names,
        operand_names[:4] + operand_names[9:],
        [pl.BlockSpec(shape), pl.BlockSpec(shape), in_hbm],
        [
            jax.ShapeDtypeStruct(shape, f32),
            jax.ShapeDtypeStruct(shape, f32),
            jax.ShapeDtypeStruct((SLOTS, VOX), bf16),
        ],
        [],
    )


def shifted(value, steps):
    axes = ("dom", "sub")
    total = lax.axis_size(axes)
    pairs = [(i, i + steps) for i in range(total) if 0 <= i + steps < total]
    return lax.ppermute(value, axes, pairs)


def body(displacement, modulus, count, points, damage, voxel):
    below = shifted(displacement, 1)
    own, low, new_damage = partition_step(
        displacement, below, modulus, count, points, damage, voxel
    )
    return own + shifted(low, -1), new_damage


def solution(mesh):
    return jax.shard_map(
        body,
        mesh=mesh,
        in_specs=(
            P(None, ("dom", "sub"), None),
            P(None, ("dom", "sub")),
            P(("dom", "sub")),
            P(("dom", "sub"), None),
            P(("dom", "sub"), None),
            P(("dom", "sub"), None),
        ),
        out_specs=(P(None, ("dom", "sub"), None), P(("dom", "sub"), None)),
        check_vma=False,
    )
```

```python
import math

import jax
import jax.numpy as jnp
import ml_dtypes
import numpy as np
from jax import lax
from jax.experimental import pallas as pl
from jax.experimental.pallas import tpu as pltpu
from jax.sharding import PartitionSpec as P

CELL = 16
EXY = 16
VOX = 4096
SLOTS = 64
GROUP = 16
LAYERS = 4
NODES = 289
WIDE = 384
ROW = EXY + 1
PAIR = 2 * GROUP
LAG = 1000
COS, SIN = 9 * GROUP, 7 * GROUP

lam_hat = 0.2 / 0.72
mu_hat = 1.0 / 2.4
ref_modulus = 2.0
kappa_sq = 4.0
law_ratio = lam_hat / (2.0 * mu_hat)
voigt_pairs = ((0, 0), (1, 1), (2, 2), (1, 2), (0, 2), (0, 1))
odd_in_x = (False, False, False, False, True, True)
table_scale = 1.132805
entry_pairs = [(k, m) for k in range(6) for m in range(k, 6)]
f32 = jnp.float32
bf16 = jnp.bfloat16
shifts = (0, 1, ROW, ROW + 1)


def shape_table():
    gauss_coord = 1.0 / math.sqrt(3.0)
    gradients = np.zeros((8, 8, 3), np.float32)
    for corner in range(8):
        signs = [2 * (corner >> d & 1) - 1 for d in range(3)]
        for gauss_no in range(8):
            coords = [(2 * (gauss_no >> d & 1) - 1) * gauss_coord for d in range(3)]
            factor = [(1.0 + signs[d] * coords[d]) / 2.0 for d in range(3)]
            for direction in range(3):
                value = float(signs[direction])
                for other in range(3):
                    if other != direction:
                        value = value * factor[other]
                gradients[corner, gauss_no, direction] = value
    return gradients


def macro_tables():
    gradients = shape_table().astype(np.float64)
    strain = np.zeros((LAYERS, 6, 8, 3, 4, 8))
    force = np.zeros((3, 4, 8, LAYERS, 6, 8))
    for layer in range(LAYERS):
        for corner in range(8):
            node_layer = layer + (corner >> 2)
            row = 4 if node_layer == 0 else node_layer - 1
            shift = corner & 3
            for k, (a, b) in enumerate(voigt_pairs):
                strain[layer, k, :, a, shift, row] += 0.5 * gradients[corner, :, b]
                strain[layer, k, :, b, shift, row] += 0.5 * gradients[corner, :, a]
                force[a, shift, row, layer, k, :] += 0.125 * gradients[corner, :, b]
                if a != b:
                    force[b, shift, row, layer, k, :] += 0.125 * gradients[corner, :, a]
    return (
        strain.reshape(LAYERS * 48, 96).astype(np.float32),
        force.reshape(96, LAYERS * 48).astype(np.float32),
    )


def spread_table():
    table = np.zeros((EXY * EXY, WIDE), np.float32)
    for y in range(EXY):
        for x in range(EXY):
            table[y * EXY + x, y * ROW + x] = 1.0
    return table


def green_matrix(n):
    n = np.asarray(n, np.float64)
    m = n @ n
    out = np.zeros((6, 6))
    if m == 0:
        return out
    lam_ref, mu_ref = ref_modulus * lam_hat, ref_modulus * mu_hat
    coupling = (lam_ref + mu_ref) / (mu_ref * (lam_ref + 2.0 * mu_ref))
    for col, (a, b) in enumerate(voigt_pairs):
        t = np.zeros((3, 3))
        t[a, b] = t[b, a] = 1.0
        u = t @ n
        amp = u / (mu_ref * m) - coupling * (n @ u) * n / m**2
        for k, (c, d) in enumerate(voigt_pairs):
            out[k, col] = 0.5 * (n[c] * amp[d] + n[d] * amp[c])
    return out


def lane_modes():
    modes = []
    for kz in range(1, 8):
        for ky in range(16):
            modes += [(ky, kz, 0), (ky, kz, 1)]
    for kz in (0, 8):
        for ky in range(1, 8):
            modes += [(ky, kz, 0), (ky, kz, 1)]
        modes += [(0, kz, 2), (8, kz, 2)]
    return modes


def spectral_tables():
    side = np.arange(16)
    modes = lane_modes()
    y, z = side.repeat(16), np.tile(side, 16)
    first = np.zeros((256, 256))
    second = np.zeros((256, 256))
    weight = np.zeros(256)
    for lane, (ky, kz, kind) in enumerate(modes):
        phase = 2 * np.pi * ((y * ky + z * kz) % 16) / 16
        first[:, lane] = np.sin(phase) if kind == 1 else np.cos(phase)
        second[:, lane] = (-np.sin(phase), np.cos(phase), np.cos(phase))[kind]
        weight[lane] = 1.0 if kind == 2 else 2.0
    rows = np.zeros((16, 16))
    row_weight = np.full(16, 2.0)
    row_weight[[0, 8]] = 1.0
    for row in range(16):
        k = row if row < 9 else row - 8
        phase = 2 * np.pi * (side * k % 16) / 16
        rows[row] = np.cos(phase) if row < 9 else np.sin(phase)

    def rounded(table):
        table = np.where(np.abs(table) < 1e-9, 0.0, table)
        return (table * table_scale).astype(ml_dtypes.bfloat16)

    eye = np.eye(GROUP)
    forward_x = rounded(np.kron(rows, eye))
    inverse_x = rounded(np.kron((rows * row_weight[:, None]).T, eye))
    signed = np.where(side < 8, side, side - 16)

    def green_at(kx, ky, kz):
        own = green_matrix((signed[kx], signed[ky], kz))
        if kz in (0, 8):
            own = (own + green_matrix((signed[-kx % 16], signed[-ky % 16], kz))) / 2
        return own

    green = np.zeros((9, len(entry_pairs), 256))
    double = np.array([1, 1, 1, 2, 2, 2])
    for kx in range(9):
        for lane, (ky, kz, kind) in enumerate(modes):
            matrix = green_at(kx, ky, kz) / double[None, :]
            green[kx, :, lane] = [matrix[pair] for pair in entry_pairs]
    scale = 2.0 * mu_hat / (table_scale**4 * VOX)
    green *= scale
    lam_ref, mu_ref = ref_modulus * lam_hat, ref_modulus * mu_hat
    coupling = (lam_ref + mu_ref) / (mu_ref * (lam_ref + 2.0 * mu_ref))
    for kx in range(9):
        for lane, (ky, kz, kind) in enumerate(modes[:128]):
            assert 0 < kz < 8
            n = np.array([signed[kx], signed[ky], kz], np.float64)
            n = n / math.sqrt(n @ n) * math.sqrt(scale / mu_ref)
            green[kx, 0:3, lane] = n
            green[kx, 3:6, lane] = n / 2
            green[kx, 6:9, lane] = n * (coupling * mu_ref**2 / scale)
    law = np.eye(6)
    law[:3, :3] += law_ratio
    uniform = np.zeros((16, 16, 6, 256))
    sign = np.where(np.array(odd_in_x), -1.0, 1.0)
    for row in range(16):
        kx = (0, 8)[row] if row < 2 else row // 2
        for lane, (ky, kz, kind) in enumerate(modes):
            matrix = green_at(kx, ky, kz) * (2.0 * mu_hat / (table_scale**4 * VOX))
            if row >= 2:
                matrix = matrix * (0.5 if row % 2 == 0 else 0.5 * sign)
            uniform[row, 0:6, :, lane] = (matrix @ law).T
    uniform = uniform.reshape(16, 16, 6 * 256)
    upper = uniform.astype(ml_dtypes.bfloat16).astype(np.float64)
    uniform[:, 6:12] = (uniform - upper)[:, 0:6]
    uniform = uniform.astype(ml_dtypes.bfloat16)
    return (
        forward_x,
        inverse_x,
        rounded(first),
        rounded(second),
        rounded((first * weight).T),
        rounded((second * weight).T),
        uniform,
        green.astype(np.float32),
    )


def dot(a, b, dims=((1,), (0,)), precision=None):
    return lax.dot_general(a, b, (dims, ((), ())), precision=precision, preferred_element_type=f32)


def split(value, parts):
    out = []
    for _ in range(parts):
        out.append(value.astype(bf16))
        value = value - out[-1].astype(f32)
    return out


def table_split(table, order):
    parts, rest = [], table.astype(np.float64)
    for _ in range(3):
        parts.append(rest.astype(ml_dtypes.bfloat16))
        rest = rest - parts[-1].astype(np.float64)
    return np.concatenate([parts[i] for i in order], axis=1)


def split_dot(table, value, order):
    parts = split(value, max(order) + 1)
    return dot(table, jnp.concatenate([parts[i] for i in order], axis=0))


half_table, half_value = (0, 1, 0), (0, 0, 1)


def strain_law(s):
    trace = lam_hat * (s[0] + s[1] + s[2])
    return [2.0 * mu_hat * s[k] + trace if k < 3 else 2.0 * mu_hat * s[k] for k in range(6)]


def half_energy(s):
    shear = s[3] * s[3] + s[4] * s[4] + s[5] * s[5]
    return s[0] * s[0] + s[1] * s[1] + s[2] * s[2] + (shear + shear)


class Cells:
    shared = ("damage", "voxel", "new", "macro", "half", "total", "matrix", "uniform", "table")
    own = ("polar", "cos", "sin", "spec_cos", "spec_sin", "green_cos", "green_sin", "plane", "field")

    def __init__(self, refs, count):
        self.count = count
        refs = list(refs)
        for name in self.shared:
            setattr(self, name, refs.pop(0))
        self.sides = [dict(zip(self.own, refs[side * 9 : side * 9 + 9])) for side in range(2)]

    @staticmethod
    def scratch():
        cos, sin, full = (6, COS, 256), (6, SIN, 256), (6, 256, 256)
        side = [
            pltpu.VMEM(full, bf16),
            pltpu.VMEM(cos, bf16),
            pltpu.VMEM(sin, bf16),
            pltpu.VMEM(cos, bf16),
            pltpu.VMEM(sin, bf16),
            pltpu.VMEM(cos, bf16),
            pltpu.VMEM(sin, bf16),
            pltpu.VMEM(full, bf16),
            pltpu.VMEM(full, f32),
        ]
        return [
            pltpu.VMEM((SLOTS, VOX), bf16),
            pltpu.VMEM((SLOTS, VOX), bf16),
            pltpu.VMEM((SLOTS, VOX), bf16),
            pltpu.VMEM((6, SLOTS, 128), f32),
            pltpu.VMEM((SLOTS, 16), bf16),
            pltpu.VMEM((6, SLOTS, 128), f32),
            pltpu.VMEM((6, 256, 256), bf16),
            pltpu.VMEM((16, 16, 6 * 256), bf16),
            pltpu.VMEM((9, len(entry_pairs), 256), f32),
            *side,
            *side,
        ]

    def solve_pair(self, pair):
        a, b = Group(self, 2 * pair, 0), Group(self, 2 * pair + 1, 1)
        in_turns(a.all_steps(), b.all_steps())


def in_turns(*works):
    works, clocks = list(works), [LAG * i for i in range(len(works))]
    while works:
        turn = clocks.index(min(clocks))
        try:
            clocks[turn] += next(works[turn])
        except StopIteration:
            del works[turn], clocks[turn]


def by_formula(nx, ny, nz, hx, hy, hz, cx, cy, cz, xx, yy, zz, yz, xz, xy):
    ux = nx * xx + hy * xy + hz * xz
    uy = ny * yy + hx * xy + hz * yz
    uz = nz * zz + hx * xz + hy * yz
    along = nx * ux + ny * uy + nz * uz
    ux, uy, uz = ux - cx * along, uy - cy * along, uz - cz * along
    return [
        *(nx * ux, ny * uy, nz * uz),
        *(hy * uz + hz * uy, hx * uz + hz * ux, hx * uy + hy * ux),
    ]


class Group:
    def __init__(self, cells, block, side):
        for name in Cells.shared:
            setattr(self, name, getattr(cells, name))
        for name, ref in cells.sides[side].items():
            setattr(self, name, ref)
        self.cells = pl.ds(pl.multiple_of(block * GROUP, GROUP), GROUP)

    def all_steps(self):
        yield from self.first_field()
        yield from self.first_green()
        yield from self.both(self.back)
        yield from self.back_x()
        yield from self.update()
        yield from self.forward()
        yield from self.green(1)
        yield from self.green(0)
        yield from self.both(self.back)
        yield from self.back_x()
        yield from self.finish()

    def back_x(self):
        for k in range(6):
            self.field[k] = dot(self.matrix[1], self.plane[k])
            yield 110

    def both(self, step):
        for i in range(2):
            yield from step(i)

    def tiles(self):
        for x in range(CELL):
            for half in range(2):
                lanes = pl.ds(half * 128, 128)
                at = pl.ds(x * 256 + half * 128, 128)
                old = self.damage[self.cells, at].astype(f32)
                young = self.voxel[self.cells, at].astype(f32)
                yield old, young, pl.ds(x * GROUP, GROUP), lanes, at

    def to_x_modes(self, k):
        both = dot(self.matrix[0], self.polar[k]).astype(bf16)
        self.cos[k] = both[:COS]
        self.sin[k] = both[COS:]

    def to_lane_modes(self, some, count):
        self.spec_cos[some] = dot(
            self.cos[some].reshape(count * COS, 256), self.matrix[2]
        ).astype(bf16).reshape(count, COS, 256)
        yield 70 * count
        self.spec_sin[some] = dot(
            self.sin[some].reshape(count * SIN, 256), self.matrix[3]
        ).astype(bf16).reshape(count, SIN, 256)
        yield 55 * count

    def first_field(self):
        macro = [self.macro[k, self.cells, :] for k in range(6)]
        whole = 1.0 / (1.0 + half_energy(macro))
        for old, young, rows, lanes, _ in self.tiles():
            excess = jnp.minimum(1.0 - old, whole) * young - ref_modulus
            self.polar[0, rows, lanes] = excess.astype(bf16)
            yield 4
        self.to_x_modes(0)
        yield 110
        yield from self.to_lane_modes(pl.ds(0, 1), 1)

    def first_green(self):
        mine = self.half[self.cells, :]
        for kx in (0, 8):
            rows = pl.ds(kx * GROUP, GROUP)
            factor = dot(mine, self.uniform[kx // 8])
            value = self.spec_cos[0, rows].astype(f32)
            for k in range(6):
                self.green_cos[k, rows] = (factor[:, k * 256 : k * 256 + 256] * value).astype(bf16)
            yield 16
        for kx in range(1, 8):
            rows, rows_sin = pl.ds(kx * GROUP, GROUP), pl.ds((kx - 1) * GROUP, GROUP)
            a, c = self.spec_cos[0, rows].astype(f32), self.spec_sin[0, rows_sin].astype(f32)
            plus, minus = a + c, a - c
            factor_plus = dot(mine, self.uniform[2 * kx])
            factor_minus = dot(mine, self.uniform[2 * kx + 1])
            for k in range(6):
                part = slice(k * 256, k * 256 + 256)
                one, two = factor_plus[:, part] * plus, factor_minus[:, part] * minus
                cos_part, sin_part = one + two, one - two
                if odd_in_x[k]:
                    cos_part, sin_part = sin_part, cos_part
                self.green_cos[k, rows] = cos_part.astype(bf16)
                self.green_sin[k, rows_sin] = sin_part.astype(bf16)
            yield 32

    def back(self, i):
        some = pl.ds(i * 3, 3)
        self.plane[some, 0:COS] = (
            dot(self.green_cos[some].reshape(3 * COS, 256), self.matrix[4])
            .astype(bf16)
            .reshape(3, COS, 256)
        )
        yield 210
        self.plane[some, COS:] = (
            dot(self.green_sin[some].reshape(3 * SIN, 256), self.matrix[5])
            .astype(bf16)
            .reshape(3, SIN, 256)
        )
        yield 165

    def strains(self, rows, lanes):
        return [self.macro[k, self.cells, :] - self.field[k, rows, lanes] for k in range(6)]

    def update(self):
        for old, young, rows, lanes, _ in self.tiles():
            s = self.strains(rows, lanes)
            kept = jnp.minimum(1.0 - old, 1.0 / (1.0 + half_energy(s))) * young
            excess = kept - ref_modulus
            double = excess + excess
            trace = law_ratio * (s[0] + s[1] + s[2])
            for k in range(6):
                value = excess * (s[k] + trace) if k < 3 else double * s[k]
                self.polar[k, rows, lanes] = value.astype(bf16)
            yield 22

    def forward(self):
        for k in range(6):
            self.to_x_modes(k)
            yield 110
        for i in range(2):
            yield from self.to_lane_modes(pl.ds(i * 3, 3), 3)

    def green(self, i):
        lanes = pl.ds(pl.multiple_of(i * 128, 128), 128)
        for kx in range(9):
            table = {}
            for entry, (k, m) in enumerate(entry_pairs):
                if kx == 0 and odd_in_x[k] != odd_in_x[m]:
                    continue
                table[k, m] = table[m, k] = self.table[kx, entry : entry + 1, lanes]

            def apply(v):
                if i == 0:
                    return by_formula(*[self.table[kx, j : j + 1, lanes] for j in range(9)], *v)
                return [
                    sum(table[k, m] * v[m] for m in range(6) if (k, m) in table) for k in range(6)
                ]

            rows = pl.ds(kx * GROUP, GROUP)
            a = [self.spec_cos[k, rows, lanes].astype(f32) for k in range(6)]
            if kx in (0, 8):
                a = apply(a)
                for k in range(6):
                    self.green_cos[k, rows, lanes] = a[k].astype(bf16)
                yield 35
                continue
            rows_sin = pl.ds((kx - 1) * GROUP, GROUP)
            c = [self.spec_sin[k, rows_sin, lanes].astype(f32) for k in range(6)]
            one = apply([c[k] if odd_in_x[k] else a[k] for k in range(6)])
            two = apply([a[k] if odd_in_x[k] else c[k] for k in range(6)])
            for k in range(6):
                cos_part, sin_part = (two, one) if odd_in_x[k] else (one, two)
                self.green_cos[k, rows, lanes] = cos_part[k].astype(bf16)
                self.green_sin[k, rows_sin, lanes] = sin_part[k].astype(bf16)
            yield 70

    def finish(self):
        sums = [jnp.zeros((GROUP, 128), f32) for k in range(6)]
        for old, young, rows, lanes, at in self.tiles():
            s = self.strains(rows, lanes)
            energy = half_energy(s)
            now = jnp.maximum(old, energy / (energy + 1.0))
            kept = (1.0 - now) * young
            sums = [sums[k] + kept * s[k] for k in range(6)]
            self.new[self.cells, at] = now.astype(bf16)
            yield 25
        for k in range(6):
            self.total[k, self.cells, :] = sums[k]
        yield 0


def macro_strain(nodes_ref, strain_ref):
    rolled = []
    for i in range(3):
        rows = nodes_ref[i]
        for shift in shifts:
            rolled.append(rows if shift == 0 else pltpu.roll(rows, WIDE - shift, 1))
    return split_dot(strain_ref[...], jnp.concatenate(rolled, axis=0), half_value)


def locate(points):
    gauss = points // (LAYERS * EXY * EXY)
    layer = points // (EXY * EXY) % LAYERS
    lane = points % (EXY * EXY) // EXY * ROW + points % EXY
    lane_no = lax.broadcasted_iota(jnp.int32, (WIDE, SLOTS), 0)
    where_at = [
        ((lane_no == lane) & (layer == z)).astype(f32).astype(bf16) for z in range(LAYERS)
    ]
    return where_at, lax.broadcasted_iota(jnp.int32, (8, SLOTS), 0) == gauss


def pick_strains(strain, where_at, is_gauss, macro_ref, half_ref):
    picked = sum(dot(strain[z * 48 : z * 48 + 48].astype(bf16), where_at[z]) for z in range(LAYERS))
    picked = jnp.where(jnp.concatenate([is_gauss] * 6, axis=0), picked, 0.0).astype(bf16)
    rows = lax.broadcasted_iota(jnp.int32, (48, 7 * 128), 0) // 8
    lanes = lax.broadcasted_iota(jnp.int32, (48, 7 * 128), 1)
    spread = jnp.where(lanes < 768, lanes // 128, (lanes - 768) % 6)
    spread = jnp.where((spread == rows) & (lanes < 768 + 12), 0.5, 0.0).astype(bf16)
    out = dot(picked, spread, ((0,), (0,)))
    for k in range(6):
        macro_ref[k] = out[:, k * 128 : k * 128 + 128]
    half_ref[...] = out[:, 768:784].astype(bf16)


def start_copies(pairs, sems):
    copies = [
        pltpu.make_async_copy(source, target, sems.at[i])
        for i, (source, target) in enumerate(pairs)
    ]
    for copy in copies:
        copy.start()

    def wait(some):
        for copy in copies[some]:
            copy.wait()

    return wait


def pier_kernel(count_ref, *refs):
    total = len(operand_names)
    sources, refs = refs[:total], refs[total:]
    own_ref, low_ref, new_hbm, *refs = refs
    targets, refs = refs[:7], refs[7:]
    in_sems, out_sems, nodes_ref, *refs = refs
    count = count_ref[0]
    cells = Cells(refs, count)
    disp_ref, below_ref, strain_ref, points_ref = targets[:4]
    modulus_ref, spread_ref, force_ref = targets[4:]
    held = dict(zip(operand_names[:4] + operand_names[9:], targets))
    held.update(
        damage=cells.damage,
        voxel=cells.voxel,
        matrix=cells.matrix,
        uniform=cells.uniform,
        green=cells.table,
    )
    early, late = [pl.ds(i * PAIR, PAIR) for i in range(2)]
    copies = [
        *[(name, None) for name in ("disp", "below", "strain", "points")],
        *[("damage", early), ("voxel", early), ("matrix", None)],
        *[("uniform", None), ("green", None), ("damage", late), ("voxel", late)],
        *[(name, None) for name in ("modulus", "spread", "force")],
    ]
    sources = dict(zip(operand_names, sources))
    copies = [
        (sources[name], held[name]) if rows is None else (sources[name].at[rows], held[name].at[rows])
        for name, rows in copies
    ]
    wait = start_copies(copies, in_sems)
    nodes_ref[...] = jnp.zeros(nodes_ref.shape, f32)
    wait(slice(0, 4))
    for i in range(3):
        nodes_ref[i, 0:LAYERS, 0:NODES] = disp_ref[i]
        nodes_ref[i, LAYERS : LAYERS + 1, 0:NODES] = below_ref[i, LAYERS - 1 : LAYERS]
    where_at, is_gauss = locate(points_ref[...])
    strain = macro_strain(nodes_ref, strain_ref)
    pick_strains(strain, where_at, is_gauss, cells.macro, cells.half)
    wait(slice(4, 9))
    busy = (count + PAIR - 1) // PAIR

    def store(pair, source):
        rows = pl.ds(pl.multiple_of(pair * PAIR, PAIR), PAIR)
        return pltpu.make_async_copy(source.at[rows], new_hbm.at[rows], out_sems.at[pair])

    @pl.loop(0, busy)
    def _(pair):
        @pl.when(pair == 1)
        def _():
            wait(slice(9, 11))

        cells.solve_pair(pair)
        rows = pl.ds(pl.multiple_of(pair * PAIR, PAIR), PAIR)
        live = lax.broadcasted_iota(jnp.int32, (PAIR, 128), 0) + pair * PAIR < count

        @pl.when((pair + 1) * PAIR > count)
        def _():
            for start in range(0, VOX, 128):
                lanes = pl.ds(start, 128)
                new, old = cells.new[rows, lanes], cells.damage[rows, lanes]
                new, old = new.astype(f32), old.astype(f32)
                cells.new[rows, lanes] = jnp.where(live, new, old).astype(bf16)

        store(pair, cells.new).start()

    @pl.loop(busy, SLOTS // PAIR)
    def _(pair):
        wait(slice(9, 11))
        store(pair, cells.damage).start()

    wait(slice(11, 14))

    slot_live = lax.broadcasted_iota(jnp.int32, (8, SLOTS), 1) < count
    at_point = is_gauss & slot_live
    ones = jnp.ones((8, 256), bf16)
    mean = [
        dot(ones, jnp.concatenate(split(cells.total[k], 2), axis=1), ((1,), (1,))) * (2.0 / VOX)
        for k in range(6)
    ]
    cell_stress = [
        jnp.where(at_point, value, 0.0).astype(bf16).astype(f32) for value in strain_law(mean)
    ]
    cell_stress.append(at_point.astype(f32))
    cell_stress = jnp.concatenate(cell_stress, axis=0).astype(bf16)
    compact = [modulus_ref[:, z * 256 : z * 256 + 256] for z in range(LAYERS)]
    young_parts = dot(jnp.concatenate(split(jnp.concatenate(compact, axis=0), 3), axis=0), spread_ref[...])
    young_all = young_parts[0:32] + young_parts[32:64] + young_parts[64:96]
    stress = []
    for z in range(LAYERS):
        young = young_all[z * 8 : z * 8 + 8]
        from_cells = dot(cell_stress, where_at[z], ((1,), (1,)))
        from_cell = from_cells[48:56] > 0.5
        elastic = strain_law([strain[z * 48 + k * 8 : z * 48 + k * 8 + 8] for k in range(6)])
        for k in range(6):
            stress.append(jnp.where(from_cell, from_cells[k * 8 : k * 8 + 8], young * elastic[k]))
    forces = split_dot(force_ref[...], jnp.concatenate(stress, axis=0), half_value)
    for i in range(3):
        total = 0.0
        for corner, shift in enumerate(shifts):
            part = forces[(i * 4 + corner) * 8 : (i * 4 + corner) * 8 + 8]
            total = total + (part if shift == 0 else pltpu.roll(part, shift, 1))
        own_ref[i] = total[0:LAYERS, 0:NODES]
        low_ref[i, 0 : LAYERS - 1] = jnp.zeros((LAYERS - 1, NODES), f32)
        low_ref[i, LAYERS - 1 : LAYERS] = total[LAYERS : LAYERS + 1, 0:NODES]


    @pl.loop(0, SLOTS // PAIR)
    def _(pair):
        store(pair, cells.new).wait()


operand_names = (
    *("disp", "below", "strain", "points", "damage", "voxel"),
    *("matrix", "uniform", "green", "modulus", "spread", "force"),
)


def call(kernel, name, count, operands, names, copied, out_specs, out_shape, scratch):
    values = [operands[key] for key in names]
    in_hbm = pl.BlockSpec(memory_space=pltpu.HBM)
    return pl.pallas_call(
        kernel,
        in_specs=[pl.BlockSpec(memory_space=pltpu.SMEM)] + [in_hbm] * len(values),
        out_specs=out_specs,
        out_shape=out_shape,
        scratch_shapes=[pltpu.VMEM(operands[key].shape, operands[key].dtype) for key in copied]
        + [pltpu.SemaphoreType.DMA((len(values) + 2,)), pltpu.SemaphoreType.DMA((4,))]
        + scratch
        + [pltpu.VMEM((3, 8, WIDE), f32)]
        + Cells.scratch(),
        compiler_params=pltpu.CompilerParams(vmem_limit_bytes=64 * 1024 * 1024),
        name=name,
    )(count, *values)


def partition_step(displacement, below, modulus, count, points, damage, voxel):
    *matrices, uniform, green = spectral_tables()
    strain, force = macro_tables()
    operands = dict(
        disp=displacement,
        below=below,
        modulus=modulus,
        points=points,
        damage=damage,
        voxel=voxel,
        matrix=jnp.asarray(np.stack(matrices)),
        uniform=jnp.asarray(uniform),
        green=jnp.asarray(green),
        strain=jnp.asarray(table_split(strain, half_table)),
        force=jnp.asarray(table_split(force, half_table)),
        spread=jnp.asarray(spread_table().astype(ml_dtypes.bfloat16)),
    )
    in_hbm = pl.BlockSpec(memory_space=pltpu.HBM)
    shape = (3, LAYERS, NODES)
    return call(
        pier_kernel,
        "pier_step",
        count,
        operands,
        operand_names,
        operand_names[:4] + operand_names[9:],
        [pl.BlockSpec(shape), pl.BlockSpec(shape), in_hbm],
        [
            jax.ShapeDtypeStruct(shape, f32),
            jax.ShapeDtypeStruct(shape, f32),
            jax.ShapeDtypeStruct((SLOTS, VOX), bf16),
        ],
        [],
    )


def shifted(value, steps):
    axes = ("dom", "sub")
    total = lax.axis_size(axes)
    pairs = [(i, i + steps) for i in range(total) if 0 <= i + steps < total]
    return lax.ppermute(value, axes, pairs)


def body(displacement, modulus, count, points, damage, voxel):
    below = shifted(displacement, 1)
    own, low, new_damage = partition_step(
        displacement, below, modulus, count, points, damage, voxel
    )
    return own + shifted(low, -1), new_damage


def solution(mesh):
    return jax.shard_map(
        body,
        mesh=mesh,
        in_specs=(
            P(None, ("dom", "sub"), None),
            P(None, ("dom", "sub")),
            P(("dom", "sub")),
            P(("dom", "sub"), None),
            P(("dom", "sub"), None),
            P(("dom", "sub"), None),
        ),
        out_specs=(P(None, ("dom", "sub"), None), P(("dom", "sub"), None)),
        check_vma=False,
    )
```
